32 devices in a mesh: parts: 2 (over y), wide: 4 (over z), narrow: 4 (over x, core).
Axes of the slice: x: 2, y: 2, z: 4, core: 2. Of those that a mesh axis runs over, the one named last changes fastest.
Arguments:
- teacher: bfloat16 [4096, 4096], P(('parts', 'wide', 'narrow')), parts along dimension 0, may hold values from -6 to 6
- weight: float32 [4096, 256], replicated, may hold values from -0.09375 to 0.09375
- block_mask: int32 [8, 4], P('parts'), parts along dimension 0, may hold values 0 or 1
- item_group: int32 [4096], P(('parts', 'wide', 'narrow')), parts along dimension 0, may hold values from 0 to 7
Outputs:
- grad_weight: float32 [8192, 256], P(('parts', 'wide', 'narrow')), parts along dimension 0
The draws below stay inside these ranges and needn't reach their ends.
There are 2 independent parts, one for each index of `parts`. The reference program is written for one: setup_inputs(seed, part) draws one part's arguments, and reference() takes and returns one part's arrays. A program takes and returns all parts, laid end to end along the dimension named above; an argument that names none is the same for every part. Nothing has to cross between parts.
Inputs may be any that keep to these rules, and one draw needn't show every extreme that they name: `block_mask`: 0 or 1 for each ordered pair of blocks.
All inputs are finite; a program needn't handle non-finite values.
Results may differ from the reference program's by a relative error of at most 0.0083.
Values may be sent and summed in bfloat16 or wider, within the bound.
No kernel may reach another device: no remote copies, remote signals or barrier semaphores. Data moves between devices by JAX's collectives and lax.ppermute only.
A program may use at most 64 MiB of HBM per device.

```python
import jax
import jax.numpy as jnp
from jax import lax

D = 4096
P_SIZE = 256
GROUPS = 8
BLOCK = 512
BLOCKS = 4
N_ITEMS = 2048


def touch_ends(result, own_key, low, largest):
    shape = result.shape
    index_at = [jax.random.randint(jax.random.fold_in(own_key, axis), (), 0, shape[axis]) for axis in range(len(shape))]
    result = result.at[tuple(index_at)].set(low)
    longest = shape.index(max(shape))
    index_at[longest] = (index_at[longest] + 1) % shape[longest]
    return result.at[tuple(index_at)].set(largest)


def block_scale(stream_key, shape, pieces, smallest, top_value):
    def one(axis_at, parts):
        heights = jax.random.uniform(jax.random.fold_in(jax.random.fold_in(stream_key, 6), axis_at), (parts,), jnp.float32, smallest / len(pieces), top_value / len(pieces))
        return jnp.repeat(jnp.exp(heights), shape[axis_at] // parts).reshape((-1,) + (1,) * (len(shape) - axis_at - 1))

    factor_of = one(*pieces[0])
    for cut in pieces[1:]:
        factor_of = factor_of * one(*cut)
    return factor_of


def normal_values(stream_key, dims, width, most, cuts=(), dtype=jnp.bfloat16):
    values = jax.random.normal(stream_key, dims, jnp.float32) * width
    if len(cuts) > 0:
        values = block_scale(stream_key, dims, cuts, -0.22, 0.18) * values
    return jnp.clip(values, min=-most, max=most).astype(dtype)


def setup_inputs(seed: int = 0, part: int = 0) -> dict:
    key_list = jax.random.split(jax.random.key(seed), 5)
    part_keys = jax.random.split(jax.random.fold_in(key_list[4], part), 5)
    return {
        "teacher": normal_values(part_keys[0], (N_ITEMS, D), 1.0, 6.0, ((0, 16),)),
        "weight": normal_values(key_list[1], (D, P_SIZE), D ** -0.5, 0.09375, (), jnp.float32),
        "block_mask": touch_ends((jax.random.randint(part_keys[2], (BLOCKS, BLOCKS), 0, 2) < 1).astype(jnp.int32), jax.random.fold_in(part_keys[2], 1), 0, 1),
        "item_group": touch_ends(jax.random.randint(part_keys[3], (N_ITEMS,), 0, GROUPS), jax.random.fold_in(part_keys[3], 1), 0, GROUPS - 1).astype(jnp.int32),
    }


def reference(teacher, weight, block_mask, item_group):
    total = teacher.shape[0]
    low_weight = weight.astype(jnp.bfloat16)
    student = jnp.dot(teacher, low_weight, preferred_element_type=jnp.float32).astype(jnp.bfloat16)
    block_of = (jnp.arange(total) // BLOCK).astype(jnp.int32)
    mask_sym = (block_mask + block_mask.T).astype(jnp.float32)
    coef = 2.0 * D / (total * P_SIZE)

    def block_rows(index):
        start = (index * BLOCK).astype(jnp.int32)
        rows_t = lax.dynamic_slice_in_dim(teacher, start, BLOCK, 0)
        rows_s = lax.dynamic_slice_in_dim(student, start, BLOCK, 0)
        rows_g = lax.dynamic_slice_in_dim(item_group, start, BLOCK, 0)
        teach = lax.dot_general(rows_t, teacher, (((1,), (1,)), ((), ())), preferred_element_type=jnp.float32) / D
        stud = lax.dot_general(rows_s, student, (((1,), (1,)), ((), ())), preferred_element_type=jnp.float32) / P_SIZE
        pair_weight = mask_sym[index][block_of]
        same = (rows_g[:, None] == item_group[None, :]).astype(jnp.float32)
        pair_term = (pair_weight[None, :] * (1.0 + same) * (stud - teach)).astype(jnp.bfloat16)
        return (coef * jnp.dot(pair_term, student, preferred_element_type=jnp.float32)).astype(jnp.bfloat16)

    grad_student = lax.map(block_rows, jnp.arange(total // BLOCK).astype(jnp.int32)).reshape(total, P_SIZE)
    return lax.dot_general(teacher, grad_student, (((0,), (0,)), ((), ())), preferred_element_type=jnp.float32)
```

```python
import functools

import jax
import jax.numpy as jnp
from jax import lax
from jax.experimental import pallas as pl
from jax.experimental.pallas import tpu as pltpu
from jax.sharding import PartitionSpec as P

ANY = pl.BlockSpec(memory_space=pl.ANY)
VMEM = pl.BlockSpec(memory_space=pltpu.VMEM)
SMEM = pl.BlockSpec(memory_space=pltpu.SMEM)
MIB = 1024 * 1024
EXTRA = 16


def swapped(value, axis, bit):
    count = lax.axis_size(axis)
    return lax.ppermute(value, axis, [(source, source ^ bit) for source in range(count)])


def in_plane(value, axis):
    found = {0: value}
    bit = lax.axis_size(axis) // 2
    while bit:
        for k in sorted(found):
            found[k ^ bit] = swapped(found[k], axis, bit)
        bit //= 2
    return [found[k] for k in sorted(found)]


def nt(a, b):
    return lax.dot_general(a, b, (((1,), (1,)), ((), ())), preferred_element_type=jnp.float32)


def loop(count, body):
    if count <= 4:
        for step in range(count):
            body(step)
    else:
        lax.fori_loop(0, count, lambda step, carry: (body(step), carry)[1], 0)


def pair_kernel(planes, lanes, rows, cols, out, width, *refs):
    pieces = planes * lanes
    panel = planes * rows
    pw = refs[0]
    t_in = refs[1 : 1 + pieces]
    s_in = refs[1 + pieces : 1 + pieces + lanes]
    outs = refs[1 + pieces + lanes : 1 + pieces + lanes + planes]
    t_all, s_all, g_raw, g_row, g_col, total, t_sem, s_sem = refs[1 + pieces + lanes + planes :]
    prow = rows + EXTRA

    def t_copy(m, k):
        at = m * planes + k
        return pltpu.make_async_copy(
            t_in[at], t_all.at[pl.ds(at * rows, rows)], t_sem.at[at]
        )

    def s_copy(m, k):
        at = m * planes + k
        return pltpu.make_async_copy(
            s_in[m].at[pl.ds(k * prow, rows)], s_all.at[pl.ds(at * rows, rows)], s_sem.at[0, at]
        )

    def g_copy(m, k):
        at = m * planes + k
        return pltpu.make_async_copy(
            s_in[m].at[pl.ds(k * prow + rows, EXTRA)],
            g_raw.at[pl.ds(at * EXTRA, EXTRA)],
            s_sem.at[1, at],
        )

    for m in range(lanes):
        for k in range(planes):
            g_copy(m, k).start()
            t_copy(m, k).start()
            s_copy(m, k).start()
    for m in range(lanes):
        for k in range(planes):
            at = m * planes + k
            g_copy(m, k).wait()
            line = g_raw[at * EXTRA : (at + 1) * EXTRA, :rows].astype(jnp.float32)[:1]
            g_row[:, at * rows : (at + 1) * rows] = jnp.broadcast_to(line, (8, rows))
            if m == 0:
                g_col[k * rows : (k + 1) * rows, :] = jnp.broadcast_to(line, (128, rows)).T
    total[...] = jnp.zeros_like(total)
    side = min(panel, 512)
    steps = panel // side
    group = side // rows

    for m in range(lanes):
        for k in range(planes):
            t_copy(m, k).wait()
            s_copy(m, k).wait()

        def one_row(it, m=m):
            at_i = pl.multiple_of(it * side, side)
            rows_t = t_all[pl.ds(at_i, side), :]
            col = g_col[pl.ds(at_i, side), :]

            def one_tile(jt):
                in_panel = pl.multiple_of(jt * side, side)
                at_j = pl.multiple_of(m * panel + jt * side, side)
                teach = nt(rows_t, t_all[pl.ds(at_j, side), :]) * (-1.0 / width)
                students = s_all[pl.ds(at_j, side), :]
                line = g_row[:1, pl.ds(at_j, side)]
                same = jnp.concatenate([col] * (side // 128), 1) == line
                terms = []
                for k in range(group):
                    weight = pw[pl.ds(it * group + k, 1), pl.ds(in_panel, side)]
                    factor = jnp.where(same[k * rows : (k + 1) * rows], 2.0 * weight, weight)
                    error = teach[k * rows : (k + 1) * rows]
                    if k == 0:
                        stud = nt(s_all[:rows, :], students) * (1.0 / out)
                        if steps > 1:
                            stud = jnp.where(it == 0, stud, 0.0)
                        error = error + stud
                    terms.append((factor * error).astype(jnp.bfloat16))
                term = jnp.concatenate(terms, 0)
                total[pl.ds(at_i, side), :] += jnp.dot(
                    term, students, preferred_element_type=jnp.float32
                )

            loop(steps, one_tile)

        loop(steps, one_row)
    for k in range(planes):
        outs[k][...] = total[k * rows : (k + 1) * rows, :].astype(outs[k].dtype)


def keep_kernel(pieces, rows, cols, lanes, lane, *refs):
    t_in, result, t_all, sem = refs[:pieces], refs[pieces], refs[pieces + 1], refs[pieces + 2]

    def copy(at):
        return pltpu.make_async_copy(t_in[at], t_all.at[pl.ds(at * rows, rows)], sem.at[at])

    for at in range(pieces):
        copy(at).start()
    for at in range(pieces):
        copy(at).wait()
    keep = cols // lanes
    for m in range(lanes):

        @pl.when(lane[0] == m)
        def _(m=m):
            result[...] = t_all[:, m * keep : (m + 1) * keep].T


def last_kernel(pieces, rows, *refs):
    t_keep, g_in, result, g_all, sem = refs[0], refs[1 : 1 + pieces], *refs[1 + pieces :]

    def copy(at):
        return pltpu.make_async_copy(g_in[at], g_all.at[pl.ds(at * rows, rows)], sem.at[at])

    for at in range(pieces):
        copy(at).start()
    for at in range(pieces):
        copy(at).wait()
    result[...] = jnp.dot(t_keep[...], g_all[...], preferred_element_type=jnp.float32)


def per_device(teacher, weight, block_mask, item_group):
    rows, width = teacher.shape
    out = weight.shape[1]
    planes = lax.axis_size("wide")
    lanes = lax.axis_size("narrow")
    plane = lax.axis_index("wide")
    lane = lax.axis_index("narrow")
    cols = width // planes
    items = rows * planes * lanes
    panel = rows * planes
    pieces = planes * lanes

    def cut(k):
        return lax.dynamic_slice_in_dim(teacher, (plane ^ k) * cols, cols, 1)

    t_parts = [cut(0)] + [swapped(cut(k), "wide", k) for k in range(1, planes)]
    low_weight = weight.astype(jnp.bfloat16)
    student = jnp.dot(teacher, low_weight, preferred_element_type=jnp.float32).astype(jnp.bfloat16)
    extra = jnp.zeros((EXTRA, out), jnp.bfloat16).at[0, :rows].set(item_group.astype(jnp.bfloat16))
    packed = jnp.concatenate([student, extra], 0)
    s_parts = [packed] + [swapped(packed, "wide", k) for k in range(1, planes)]

    t_all = [in_plane(t, "narrow") for t in t_parts]
    t_all = [t_all[k][m] for m in range(lanes) for k in range(planes)]
    s_all = in_plane(jnp.concatenate(s_parts, 0), "narrow")

    sym = (block_mask + block_mask.T).astype(jnp.float32)
    order = plane ^ jnp.arange(planes)
    sym = jnp.take(jnp.take(sym, order, 0), order, 1)
    pair_weight = jnp.repeat(sym, rows, 1)
    parts = pl.pallas_call(
        functools.partial(pair_kernel, planes, lanes, rows, cols, out, width),
        out_shape=[jax.ShapeDtypeStruct((rows, out), jnp.float32)]
        + [jax.ShapeDtypeStruct((rows, out), jnp.bfloat16)] * (planes - 1),
        in_specs=[VMEM] + [ANY] * (pieces + lanes),
        out_specs=[VMEM] * planes,
        scratch_shapes=[
            pltpu.VMEM((items, cols), jnp.bfloat16),
            pltpu.VMEM((items, out), jnp.bfloat16),
            pltpu.VMEM((pieces * EXTRA, out), jnp.bfloat16),
            pltpu.VMEM((8, items), jnp.float32),
            pltpu.VMEM((panel, 128), jnp.float32),
            pltpu.VMEM((panel, out), jnp.float32),
            pltpu.SemaphoreType.DMA((pieces,)),
            pltpu.SemaphoreType.DMA((2, pieces)),
        ],
        compiler_params=pltpu.CompilerParams(vmem_limit_bytes=44 * MIB),
        cost_estimate=pl.CostEstimate(
            flops=2 * panel * items * (cols + out),
            bytes_accessed=2 * items * (cols + out),
            transcendentals=0,
        ),
        name="pairs",
    )(pair_weight, *t_all, *s_all)

    keep = cols // lanes
    t_keep = pl.pallas_call(
        functools.partial(keep_kernel, pieces, rows, cols, lanes),
        out_shape=jax.ShapeDtypeStruct((keep, items), jnp.bfloat16),
        in_specs=[SMEM] + [ANY] * pieces,
        out_specs=VMEM,
        scratch_shapes=[
            pltpu.VMEM((items, cols), jnp.bfloat16),
            pltpu.SemaphoreType.DMA((pieces,)),
        ],
        compiler_params=pltpu.CompilerParams(vmem_limit_bytes=32 * MIB),
        cost_estimate=pl.CostEstimate(
            flops=0, bytes_accessed=2 * items * (cols + keep), transcendentals=0
        ),
        name="keep",
    )(lane.astype(jnp.int32).reshape(1), *t_all)

    mine = parts[0]
    for k in range(1, planes):
        mine = mine + swapped(parts[k], "wide", k).astype(jnp.float32)
    coef = 2.0 * width / (items * out)
    grad = (mine * coef).astype(jnp.bfloat16)
    g_parts = [grad] + [swapped(grad, "wide", k) for k in range(1, planes)]
    first = in_plane(grad, "narrow")
    rest = in_plane(jnp.concatenate(g_parts[1:], 0), "narrow")
    g_all = []
    for m in range(lanes):
        g_all.append(first[m])
        for k in range(planes - 1):
            g_all.append(rest[m][k * rows : (k + 1) * rows])
    return pl.pallas_call(
        functools.partial(last_kernel, pieces, rows),
        out_shape=jax.ShapeDtypeStruct((keep, out), jnp.float32),
        in_specs=[VMEM] + [ANY] * pieces,
        out_specs=VMEM,
        scratch_shapes=[
            pltpu.VMEM((items, out), jnp.bfloat16),
            pltpu.SemaphoreType.DMA((pieces,)),
        ],
        compiler_params=pltpu.CompilerParams(vmem_limit_bytes=24 * MIB),
        cost_estimate=pl.CostEstimate(
            flops=2 * items * keep * out, bytes_accessed=2 * items * (keep + out), transcendentals=0
        ),
        name="last",
    )(t_keep, *g_all)


def solution(mesh):
    in_specs = (
        P(("parts", "wide", "narrow"), None),
        P(),
        P("parts", None),
        P(("parts", "wide", "narrow")),
    )
    out_specs = P(("parts", "wide", "narrow"), None)
    return jax.shard_map(
        per_device, mesh=mesh, in_specs=in_specs, out_specs=out_specs, check_vma=False
    )
```

```python
import functools

import jax
import jax.numpy as jnp
from jax import lax
from jax.experimental import pallas as pl
from jax.experimental.pallas import tpu as pltpu
from jax.sharding import PartitionSpec as P

ANY = pl.BlockSpec(memory_space=pl.ANY)
VMEM = pl.BlockSpec(memory_space=pltpu.VMEM)
SMEM = pl.BlockSpec(memory_space=pltpu.SMEM)
MIB = 1024 * 1024
EXTRA = 16
FAR, CORE = 2, 1


def swapped(value, axis, bit):
    count = lax.axis_size(axis)
    return lax.ppermute(value, axis, [(source, source ^ bit) for source in range(count)])


def after(value, *others):
    return lax.optimization_barrier((value, *others))[0]


def vmem_room(held):
    return held + 14 * MIB


def cost(flops, moved):
    return pl.CostEstimate(flops=flops, bytes_accessed=moved, transcendentals=0)


def nt(a, b):
    return lax.dot_general(a, b, (((1,), (1,)), ((), ())), preferred_element_type=jnp.float32)


def loop(count, body):
    if count <= 4:
        for step in range(count):
            body(step)
    else:
        lax.fori_loop(0, count, lambda step, carry: (body(step), carry)[1], 0)


def student_kernel(steps, teacher, weight, group, packed, t_all, w_all, t_sem, w_sem):
    rows, width = teacher.shape
    out = weight.shape[1]
    depth = width // steps

    def w_copy(step):
        part = pl.ds(step * depth, depth)
        return pltpu.make_async_copy(weight.at[part], w_all.at[part], w_sem.at[step])

    def t_copy(step):
        part = pl.ds(step * depth, depth)
        return pltpu.make_async_copy(teacher.at[:, part], t_all.at[:, part], t_sem.at[step])

    for step in range(steps):
        t_copy(step).start()
        w_copy(step).start()
    line = jnp.broadcast_to(group[...].astype(jnp.float32), (EXTRA, rows))
    packed[rows:, :rows] = line.astype(jnp.bfloat16)
    total = jnp.zeros((rows, out), jnp.float32)
    for step in range(steps):
        t_copy(step).wait()
        w_copy(step).wait()
        total += jnp.dot(
            t_all[:, step * depth : (step + 1) * depth],
            w_all[step * depth : (step + 1) * depth, :].astype(jnp.bfloat16),
            preferred_element_type=jnp.float32,
        )
    packed[:rows, :] = total.astype(jnp.bfloat16)


def pair_kernel(planes, lanes, rows, out, width, own, mask, place, *refs):
    pieces = planes * lanes
    panel = planes * rows
    prow = rows + EXTRA
    t_in, s_in = refs[:pieces], refs[pieces : pieces + lanes]
    result = refs[pieces + lanes]
    rest = list(refs[pieces + lanes + 1 :])
    t_keep = rest.pop(0) if own else None
    t_all, s_all, g_raw, g_row, g_col, total, t_sem, s_sem, g_sem = rest
    here = place[0]
    lead = 0 if own else FAR

    def t_copy(m, k):
        at = m * planes + k
        return pltpu.make_async_copy(t_in[at], t_all.at[pl.ds(at * rows, rows)], t_sem.at[at])

    def s_copy(m, k):
        at = m * planes + k
        return pltpu.make_async_copy(
            s_in[m].at[pl.ds(k * prow, rows)], s_all.at[pl.ds(at * rows, rows)], s_sem.at[at]
        )

    def g_copy(m, k):
        at = m * planes + k
        return pltpu.make_async_copy(
            s_in[m].at[pl.ds(k * prow + rows, EXTRA)],
            g_raw.at[pl.ds(at * EXTRA, EXTRA)],
            g_sem.at[at],
        )

    order = [lead] + [m for m in range(lanes) if m != lead]
    for m in order:
        for k in range(planes):
            for copy in (g_copy(m, k), t_copy(m, k), s_copy(m, k)):
                copy.start()
    for m in order:
        for k in range(planes):
            at = m * planes + k
            g_copy(m, k).wait()
            line = g_raw[at * EXTRA : (at + 1) * EXTRA, :rows].astype(jnp.float32)[:1]
            g_row[:, at * rows : (at + 1) * rows] = jnp.broadcast_to(line, (8, rows))
            if m == lead:
                g_col[k * rows : (k + 1) * rows, :] = jnp.broadcast_to(line, (128, rows)).T
    total[...] = jnp.zeros_like(total)
    side = min(panel, 512)
    steps = panel // side
    group = side // rows

    for m in order:
        for k in range(planes):
            t_copy(m, k).wait()
            s_copy(m, k).wait()

        def one_row(it, m=m):
            at_i = pl.multiple_of(it * side, side)
            rows_t = t_all[pl.ds(lead * panel + at_i, side), :]
            col = g_col[pl.ds(at_i, side), :]

            def one_tile(jt):
                at_j = pl.multiple_of(m * panel + jt * side, side)
                teach = nt(rows_t, t_all[pl.ds(at_j, side), :]) * (-1.0 / width)
                students = s_all[pl.ds(at_j, side), :]
                line = g_row[:1, pl.ds(at_j, side)]
                same = jnp.concatenate([col] * (side // 128), 1) == line
                terms = []
                for k in range(group):
                    mine = here ^ (it * group + k)
                    weights = []
                    for other in range(group):
                        theirs = here ^ (jt * group + other)
                        both = mask[mine, theirs] + mask[theirs, mine]
                        weights.append(jnp.full((1, rows), both.astype(jnp.float32)))
                    weight = jnp.concatenate(weights, 1)
                    factor = jnp.where(same[k * rows : (k + 1) * rows], 2.0 * weight, weight)
                    error = teach[k * rows : (k + 1) * rows]
                    if own and k == 0:
                        stud = nt(s_all[:rows, :], students) * (1.0 / out)
                        if steps > 1:
                            stud = jnp.where(it == 0, stud, 0.0)
                        error = error + stud
                    terms.append((factor * error).astype(jnp.bfloat16))
                term = jnp.concatenate(terms, 0)
                total[pl.ds(at_i, side), :] += jnp.dot(
                    term, students, preferred_element_type=jnp.float32
                )

            loop(steps, one_tile)

        loop(steps, one_row)
    result[...] = total[...].astype(result.dtype)
    if own:
        keep = t_keep.shape[1]
        for c in range(2):

            @pl.when(place[1] % 2 == c)
            def _(c=c):
                t_keep[...] = t_all[:, c * keep : (c + 1) * keep]


def pair_values_kernel(planes, lanes, rows, out, width, own, mask, place, *refs):
    pieces = planes * lanes
    prow = rows + EXTRA
    t_in, s_in = refs[:pieces], refs[pieces : pieces + lanes]
    result = refs[pieces + lanes]
    here = place[0]
    lead = 0 if own else FAR

    def joined(parts, axis=0):
        return jnp.concatenate(list(parts), axis)

    def panel_of(m):
        return joined(t_in[m * planes + k][...] for k in range(planes))

    def students_of(m):
        return joined(s_in[m][k * prow : k * prow + rows, :] for k in range(planes))

    def groups_of(m, k):
        at = k * prow + rows
        return s_in[m][at : at + EXTRA, :rows].astype(jnp.float32)[:1]

    weights = []
    for k in range(planes):
        scalars = [mask[here ^ k, here ^ j] + mask[here ^ j, here ^ k] for j in range(planes)]
        line = [jnp.full((1, rows), one.astype(jnp.float32) * (-1.0 / width)) for one in scalars]
        weights.append(joined(line, 1))
    column = joined(jnp.broadcast_to(groups_of(lead, k), (128, rows)).T for k in range(planes))
    column = joined([column] * (planes * rows // 128), 1)
    lead_t = panel_of(lead)
    total = jnp.zeros((planes * rows, out), jnp.float32)
    for m in [lead] + [m for m in range(lanes) if m != lead]:
        students = students_of(m)
        teach = nt(lead_t, panel_of(m))
        same = column == joined((groups_of(m, k) for k in range(planes)), 1)
        terms = []
        for k in range(planes):
            error = teach[k * rows : (k + 1) * rows]
            if own and k == 0:
                error = error - nt(s_in[0][:rows, :], students) * (width / out)
            factor = jnp.where(same[k * rows : (k + 1) * rows], 2.0 * weights[k], weights[k])
            terms.append((factor * error).astype(jnp.bfloat16))
        total = total + jnp.dot(joined(terms), students, preferred_element_type=jnp.float32)
    result[...] = total.astype(result.dtype)
    if own:
        t_keep = refs[pieces + lanes + 1]
        keep = t_keep.shape[1]
        for c in range(2):

            @pl.when(place[1] % 2 == c)
            def _(c=c):
                for at in range(pieces):
                    t_keep[at * rows : (at + 1) * rows, :] = t_in[at][:, c * keep : (c + 1) * keep]


def flip_kernel(value, result):
    result[...] = value[...].T


def last_kernel(planes, lanes, rows, t_keep, *refs):
    g_in, result = refs[:4], refs[4]
    total = None
    for at in range(4):
        count = 1 if at < 2 else planes - 1
        for far in range(lanes // 2):
            first = (2 * far + at % 2) * planes + (at >= 2)
            one = jnp.dot(
                t_keep[:, first * rows : (first + count) * rows],
                g_in[at][far * count * rows : (far + 1) * count * rows, :],
                preferred_element_type=jnp.float32,
            )
            total = one if total is None else total + one
    result[...] = total


def per_device(teacher, weight, block_mask, item_group):
    rows, width = teacher.shape
    out = weight.shape[1]
    planes = lax.axis_size("wide")
    lanes = lax.axis_size("narrow")
    plane = lax.axis_index("wide")
    lane = lax.axis_index("narrow")
    cols = width // planes
    part = cols // 2
    keep = cols // lanes
    items = rows * planes * lanes
    panel = rows * planes
    pieces = planes * lanes
    here = jnp.stack([plane, lane]).astype(jnp.int32)
    half = planes // 2

    def cut(k, side):
        start = (plane ^ k) * cols + (lane // 2 ^ side) * part
        return lax.dynamic_slice_in_dim(teacher, start, part, 1)

    mine = [cut(k, 0) for k in range(planes)]
    theirs_far = jnp.concatenate([cut(k, 1) for k in range(half, planes)], 0)
    theirs_near = jnp.concatenate([cut(k, 1) for k in range(half)], 0)
    got_far = swapped(theirs_far, "narrow", FAR)
    got_near = swapped(after(theirs_near, got_far), "narrow", FAR)
    got = [
        (got_near, got_far)[k >= half][k % half * rows : (k % half + 1) * rows] for k in range(planes)
    ]
    first = [mine[0]] + [swapped(mine[k], "wide", k) for k in range(1, planes)]
    second = [got[0]] + [swapped(got[k], "wide", k) for k in range(1, planes)]

    steps = 8
    packed = pl.pallas_call(
        functools.partial(student_kernel, steps),
        out_shape=jax.ShapeDtypeStruct((rows + EXTRA, out), jnp.bfloat16),
        in_specs=[ANY, ANY, VMEM],
        out_specs=VMEM,
        scratch_shapes=[
            pltpu.VMEM((rows, width), jnp.bfloat16),
            pltpu.VMEM((width, out), jnp.float32),
            pltpu.SemaphoreType.DMA((steps,)),
            pltpu.SemaphoreType.DMA((steps,)),
        ],
        compiler_params=pltpu.CompilerParams(vmem_limit_bytes=56 * MIB),
        cost_estimate=cost(2 * rows * width * out, width * (2 * rows + 4 * out)),
        name="student",
    )(after(teacher, theirs_far), weight, item_group.reshape(1, rows))
    s_own = [packed] + [swapped(packed, "wide", k) for k in range(1, planes)]
    s_own = jnp.concatenate(s_own, 0)
    s_far = swapped(s_own, "narrow", FAR)
    s_all = [s_own, swapped(s_own, "narrow", CORE), s_far, swapped(s_far, "narrow", CORE)]

    t_all = [*first, *(swapped(t, "narrow", CORE) for t in first)]
    t_all += [*second, *(swapped(t, "narrow", CORE) for t in second)]

    def pairs(own):
        shapes = [jax.ShapeDtypeStruct((panel, out), jnp.float32 if own else jnp.bfloat16)]
        if own:
            shapes.append(jax.ShapeDtypeStruct((items, keep), jnp.bfloat16))
        held = items * (2 * part + 2 * out) + 4 * panel * out
        if pieces <= 16 and panel <= 512:
            return pl.pallas_call(
                functools.partial(pair_values_kernel, planes, lanes, rows, out, width, own),
                out_shape=shapes,
                in_specs=[SMEM, SMEM] + [VMEM] * (pieces + lanes),
                out_specs=[VMEM] * len(shapes),
                compiler_params=pltpu.CompilerParams(vmem_limit_bytes=vmem_room(held)),
                cost_estimate=cost(2 * panel * items * (part + out), 2 * items * (part + out)),
                name="pairs_own" if own else "pairs_far",
            )(block_mask, here, *t_all, *s_all)
        return pl.pallas_call(
            functools.partial(pair_kernel, planes, lanes, rows, out, width, own),
            out_shape=shapes,
            in_specs=[SMEM, SMEM] + [ANY] * (pieces + lanes),
            out_specs=[VMEM] * len(shapes),
            scratch_shapes=[
                pltpu.VMEM((items, part), jnp.bfloat16),
                pltpu.VMEM((items, out), jnp.bfloat16),
                pltpu.VMEM((pieces * EXTRA, out), jnp.bfloat16),
                pltpu.VMEM((8, items), jnp.float32),
                pltpu.VMEM((panel, 128), jnp.float32),
                pltpu.VMEM((panel, out), jnp.float32),
                pltpu.SemaphoreType.DMA((pieces,)),
                pltpu.SemaphoreType.DMA((pieces,)),
                pltpu.SemaphoreType.DMA((pieces,)),
            ],
            compiler_params=pltpu.CompilerParams(vmem_limit_bytes=vmem_room(held)),
            cost_estimate=cost(2 * panel * items * (part + out), 2 * items * (part + out)),
            name="pairs_own" if own else "pairs_far",
        )(block_mask, here, *t_all, *s_all)

    (far_sum,) = pairs(False)
    far_sum = swapped(far_sum, "narrow", FAR)
    own_sum, t_keep = pairs(True)
    sums = own_sum + far_sum.astype(jnp.float32)
    t_keep = pl.pallas_call(
        flip_kernel,
        out_shape=jax.ShapeDtypeStruct((keep, items), jnp.bfloat16),
        in_specs=[VMEM],
        out_specs=VMEM,
        compiler_params=pltpu.CompilerParams(vmem_limit_bytes=vmem_room(4 * items * keep)),
        cost_estimate=cost(0, 4 * items * keep),
        name="flip",
    )(t_keep)

    grad = after(sums[:rows], t_keep)
    for k in range(1, planes):
        piece = sums[k * rows : (k + 1) * rows].astype(jnp.bfloat16)
        grad = grad + swapped(piece, "wide", k).astype(jnp.float32)
    coef = 2.0 * width / (items * out)
    grad = (grad * coef).astype(jnp.bfloat16)
    g_parts = [swapped(grad, "wide", k) for k in range(1, planes)]
    g_near = jnp.concatenate([grad, swapped(grad, "narrow", FAR)], 0)
    g_rest = after(jnp.concatenate(g_parts, 0), g_near)
    g_rest = jnp.concatenate([g_rest, swapped(g_rest, "narrow", FAR)], 0)
    g_all = [g_near, swapped(g_near, "narrow", CORE), g_rest, swapped(g_rest, "narrow", CORE)]
    return pl.pallas_call(
        functools.partial(last_kernel, planes, lanes, rows),
        out_shape=jax.ShapeDtypeStruct((keep, out), jnp.float32),
        in_specs=[VMEM] * 5,
        out_specs=VMEM,
        compiler_params=pltpu.CompilerParams(vmem_limit_bytes=vmem_room(4 * items * (out + keep))),
        cost_estimate=cost(2 * items * keep * out, 2 * items * (keep + out)),
        name="last",
    )(t_keep, *g_all)


def solution(mesh):
    in_specs = (
        P(("parts", "wide", "narrow"), None),
        P(),
        P("parts", None),
        P(("parts", "wide", "narrow")),
    )
    out_specs = P(("parts", "wide", "narrow"), None)
    return jax.shard_map(
        per_device, mesh=mesh, in_specs=in_specs, out_specs=out_specs, check_vma=False
    )
```

```python
import functools

import jax
import jax.numpy as jnp
from jax import lax
from jax.experimental import pallas as pl
from jax.experimental.pallas import tpu as pltpu
from jax.sharding import PartitionSpec as P

ANY = pl.BlockSpec(memory_space=pl.ANY)
VMEM = pl.BlockSpec(memory_space=pltpu.VMEM)
SMEM = pl.BlockSpec(memory_space=pltpu.SMEM)
MIB = 1024 * 1024
EXTRA = 16
FAR, CORE = 2, 1
HELD = 72_000_000
NEAR = 2


def swapped(value, axis, bit):
    count = lax.axis_size(axis)
    return lax.ppermute(value, axis, [(source, source ^ bit) for source in range(count)])


def after(value, *others):
    return lax.optimization_barrier((value, *others))[0]


def vmem_room(held):
    return held + 14 * MIB


def cost(flops, moved):
    return pl.CostEstimate(flops=flops, bytes_accessed=moved, transcendentals=0)


def nt(a, b):
    return lax.dot_general(a, b, (((1,), (1,)), ((), ())), preferred_element_type=jnp.float32)


def loop(count, body):
    if count <= 4:
        for step in range(count):
            body(step)
    else:
        lax.fori_loop(0, count, lambda step, carry: (body(step), carry)[1], 0)


def student_kernel(steps, teacher, weight, group, packed, t_all, w_all, t_sem, w_sem):
    rows, width = teacher.shape
    out = weight.shape[1]
    depth = width // steps

    def w_copy(step):
        part = pl.ds(step * depth, depth)
        return pltpu.make_async_copy(weight.at[part], w_all.at[part], w_sem.at[step])

    def t_copy(step):
        part = pl.ds(step * depth, depth)
        return pltpu.make_async_copy(teacher.at[:, part], t_all.at[:, part], t_sem.at[step])

    for step in range(steps):
        t_copy(step).start()
        w_copy(step).start()
    line = jnp.broadcast_to(group[...].astype(jnp.float32), (EXTRA, rows))
    packed[rows:, :rows] = line.astype(jnp.bfloat16)
    total = jnp.zeros((rows, out), jnp.float32)
    for step in range(steps):
        t_copy(step).wait()
        w_copy(step).wait()
        total += jnp.dot(
            t_all[:, step * depth : (step + 1) * depth],
            w_all[step * depth : (step + 1) * depth, :].astype(jnp.bfloat16),
            preferred_element_type=jnp.float32,
        )
    packed[:rows, :] = total.astype(jnp.bfloat16)


def pair_kernel(planes, lanes, rows, out, width, own, mask, place, *refs):
    pieces = planes * lanes
    panel = planes * rows
    prow = rows + EXTRA
    t_in, s_in = refs[:pieces], refs[pieces : pieces + 2 * lanes]
    result = refs[pieces + 2 * lanes]
    rest = list(refs[pieces + 2 * lanes + 1 :])
    t_keep = rest.pop(0) if own else None
    t_all, s_all, g_raw, g_row, g_col, total, t_sem, s_sem, g_sem = rest
    here = place[0]
    lead = 0 if own else FAR

    def t_copy(m, k):
        at = m * planes + k
        return pltpu.make_async_copy(t_in[at], t_all.at[pl.ds(at * rows, rows)], t_sem.at[at])

    def s_part(m, k, first, count):
        late = k >= NEAR
        return s_in[2 * m + late].at[pl.ds((k - late * NEAR) * prow + first, count)]

    def s_copy(m, k):
        at = m * planes + k
        return pltpu.make_async_copy(
            s_part(m, k, 0, rows), s_all.at[pl.ds(at * rows, rows)], s_sem.at[at]
        )

    def g_copy(m, k):
        at = m * planes + k
        return pltpu.make_async_copy(
            s_part(m, k, rows, EXTRA),
            g_raw.at[pl.ds(at * EXTRA, EXTRA)],
            g_sem.at[at],
        )

    order = [lead] + [m for m in range(lanes) if m != lead]
    for m in order:
        for k in range(planes):
            for copy in (g_copy(m, k), t_copy(m, k), s_copy(m, k)):
                copy.start()
    for m in order:
        for k in range(planes):
            at = m * planes + k
            g_copy(m, k).wait()
            line = g_raw[at * EXTRA : (at + 1) * EXTRA, :rows].astype(jnp.float32)[:1]
            g_row[:, at * rows : (at + 1) * rows] = jnp.broadcast_to(line, (8, rows))
            if m == lead:
                g_col[k * rows : (k + 1) * rows, :] = jnp.broadcast_to(line, (128, rows)).T
    total[...] = jnp.zeros_like(total)
    side = min(panel, 512)
    steps = panel // side
    group = side // rows

    for m in order:
        for k in range(planes):
            t_copy(m, k).wait()
            s_copy(m, k).wait()

        def one_row(it, m=m):
            at_i = pl.multiple_of(it * side, side)
            rows_t = t_all[pl.ds(lead * panel + at_i, side), :]
            col = g_col[pl.ds(at_i, side), :]

            def one_tile(jt):
                at_j = pl.multiple_of(m * panel + jt * side, side)
                teach = nt(rows_t, t_all[pl.ds(at_j, side), :]) * (-1.0 / width)
                students = s_all[pl.ds(at_j, side), :]
                line = g_row[:1, pl.ds(at_j, side)]
                same = jnp.concatenate([col] * (side // 128), 1) == line
                terms = []
                for k in range(group):
                    mine = here ^ (it * group + k)
                    weights = []
                    for other in range(group):
                        theirs = here ^ (jt * group + other)
                        both = mask[mine, theirs] + mask[theirs, mine]
                        weights.append(jnp.full((1, rows), both.astype(jnp.float32)))
                    weight = jnp.concatenate(weights, 1)
                    factor = jnp.where(same[k * rows : (k + 1) * rows], 2.0 * weight, weight)
                    error = teach[k * rows : (k + 1) * rows]
                    if own and k == 0:
                        stud = nt(s_all[:rows, :], students) * (1.0 / out)
                        if steps > 1:
                            stud = jnp.where(it == 0, stud, 0.0)
                        error = error + stud
                    terms.append((factor * error).astype(jnp.bfloat16))
                term = jnp.concatenate(terms, 0)
                total[pl.ds(at_i, side), :] += jnp.dot(
                    term, students, preferred_element_type=jnp.float32
                )

            loop(steps, one_tile)

        loop(steps, one_row)
    result[...] = total[...].astype(result.dtype)
    if own:
        keep = t_keep.shape[1]
        for c in range(2):

            @pl.when(place[1] % 2 == c)
            def _(c=c):
                t_keep[...] = t_all[:, c * keep : (c + 1) * keep]


def pair_values_kernel(planes, lanes, rows, out, width, own, mask, place, *refs):
    pieces = planes * lanes
    prow = rows + EXTRA
    t_in, s_in = refs[:pieces], refs[pieces : pieces + 2 * lanes]
    result = refs[pieces + 2 * lanes]
    here = place[0]
    lead = 0 if own else FAR

    def joined(parts, axis=0):
        return jnp.concatenate(list(parts), axis)

    def panel_of(m):
        return joined(t_in[m * planes + k][...] for k in range(planes))

    def s_part(m, k, first, count):
        late = k >= NEAR
        at = (k - late * NEAR) * prow + first
        return s_in[2 * m + late][at : at + count, :]

    def students_of(m):
        return joined(s_part(m, k, 0, rows) for k in range(planes))

    def groups_of(m, k):
        return s_part(m, k, rows, EXTRA)[:, :rows].astype(jnp.float32)[:1]

    weights = []
    for k in range(planes):
        scalars = [mask[here ^ k, here ^ j] + mask[here ^ j, here ^ k] for j in range(planes)]
        line = [jnp.full((1, rows), one.astype(jnp.float32) * (-1.0 / width)) for one in scalars]
        weights.append(joined(line, 1))
    column = joined(jnp.broadcast_to(groups_of(lead, k), (128, rows)).T for k in range(planes))
    column = joined([column] * (planes * rows // 128), 1)
    lead_t = panel_of(lead)
    total = jnp.zeros((planes * rows, out), jnp.float32)
    for m in [lead] + [m for m in range(lanes) if m != lead]:
        students = students_of(m)
        teach = nt(lead_t, panel_of(m))
        same = column == joined((groups_of(m, k) for k in range(planes)), 1)
        terms = []
        for k in range(planes):
            error = teach[k * rows : (k + 1) * rows]
            if own and k == 0:
                error = error - nt(s_in[0][:rows, :], students) * (width / out)
            factor = jnp.where(same[k * rows : (k + 1) * rows], 2.0 * weights[k], weights[k])
            terms.append((factor * error).astype(jnp.bfloat16))
        total = total + jnp.dot(joined(terms), students, preferred_element_type=jnp.float32)
    result[...] = total.astype(result.dtype)
    if own:
        t_keep = refs[pieces + 2 * lanes + 1]
        keep = t_keep.shape[1]
        for c in range(2):

            @pl.when(place[1] % 2 == c)
            def _(c=c):
                for at in range(pieces):
                    t_keep[at * rows : (at + 1) * rows, :] = t_in[at][:, c * keep : (c + 1) * keep]


def hold_kernel(*refs):
    half = len(refs) // 2
    for source, target in zip(refs[:half], refs[half:]):
        target[...] = source[...]


def flip_kernel(value, result):
    result[...] = value[...].T


def last_kernel(planes, lanes, rows, t_keep, *refs):
    g_in, result = refs[:4], refs[4]
    total = None
    for at in range(4):
        count = 1 if at < 2 else planes - 1
        for far in range(lanes // 2):
            first = (2 * far + at % 2) * planes + (at >= 2)
            one = jnp.dot(
                t_keep[:, first * rows : (first + count) * rows],
                g_in[at][far * count * rows : (far + 1) * count * rows, :],
                preferred_element_type=jnp.float32,
            )
            total = one if total is None else total + one
    result[...] = total


def per_device(teacher, weight, block_mask, item_group):
    rows, width = teacher.shape
    out = weight.shape[1]
    planes = lax.axis_size("wide")
    lanes = lax.axis_size("narrow")
    plane = lax.axis_index("wide")
    lane = lax.axis_index("narrow")
    cols = width // planes
    part = cols // 2
    keep = cols // lanes
    items = rows * planes * lanes
    panel = rows * planes
    pieces = planes * lanes
    here = jnp.stack([plane, lane]).astype(jnp.int32)
    half = planes // 2

    def cut(k, side):
        start = (plane ^ k) * cols + (lane // 2 ^ side) * part
        return lax.dynamic_slice_in_dim(teacher, start, part, 1)

    mine = [cut(k, 0) for k in range(planes)]
    theirs = jnp.concatenate([cut(k, 1) for k in range(planes)], 0)
    got = swapped(theirs, "narrow", FAR)
    got = [got[k * rows : (k + 1) * rows] for k in range(planes)]
    own_core = swapped(mine[0], "narrow", CORE)
    first = [mine[0]] + [swapped(mine[k], "wide", k) for k in range(1, planes)]
    second = [got[0]] + [swapped(got[k], "wide", k) for k in range(1, planes)]

    steps = 8
    packed = pl.pallas_call(
        functools.partial(student_kernel, steps),
        out_shape=jax.ShapeDtypeStruct((rows + EXTRA, out), jnp.bfloat16),
        in_specs=[ANY, ANY, VMEM],
        out_specs=VMEM,
        scratch_shapes=[
            pltpu.VMEM((rows, width), jnp.bfloat16),
            pltpu.VMEM((width, out), jnp.float32),
            pltpu.SemaphoreType.DMA((steps,)),
            pltpu.SemaphoreType.DMA((steps,)),
        ],
        compiler_params=pltpu.CompilerParams(vmem_limit_bytes=56 * MIB),
        cost_estimate=cost(2 * rows * width * out, width * (2 * rows + 4 * out)),
        name="student",
    )(after(teacher, own_core), weight, item_group.reshape(1, rows))
    s_of = {0: packed}
    bit = half
    while bit:
        for k in sorted(s_of):
            s_of[k ^ bit] = swapped(s_of[k], "wide", bit)
        bit //= 2
    s_all = [None] * lanes * 2
    for part_at, odd in enumerate((0, 1)):
        own = jnp.concatenate([s_of[k] for k in range(planes) if (k >= NEAR) == odd], 0)
        far = swapped(own, "narrow", FAR)
        for m, value in ((0, own), (FAR, far)):
            s_all[2 * m + part_at] = value
            s_all[2 * (m ^ CORE) + part_at] = swapped(value, "narrow", CORE)

    t_all = [*first, own_core, *(swapped(t, "narrow", CORE) for t in first[1:])]
    t_all += [*second, *(swapped(t, "narrow", CORE) for t in second)]

    late = 2 * planes
    t_all[late:] = pl.pallas_call(
        hold_kernel,
        out_shape=[jax.ShapeDtypeStruct((rows, part), jnp.bfloat16)] * late,
        in_specs=[VMEM] * late,
        out_specs=[VMEM] * late,
        compiler_params=pltpu.CompilerParams(vmem_limit_bytes=vmem_room(8 * late * rows * part)),
        cost_estimate=cost(0, HELD),
        name="hold",
    )(*t_all[late:])

    def pairs(own):
        shapes = [jax.ShapeDtypeStruct((panel, out), jnp.float32 if own else jnp.bfloat16)]
        if own:
            shapes.append(jax.ShapeDtypeStruct((items, keep), jnp.bfloat16))
        held = items * (2 * part + 2 * out) + 4 * panel * out
        if pieces <= 16 and panel <= 512:
            return pl.pallas_call(
                functools.partial(pair_values_kernel, planes, lanes, rows, out, width, own),
                out_shape=shapes,
                in_specs=[SMEM, SMEM] + [VMEM] * (pieces + 2 * lanes),
                out_specs=[VMEM] * len(shapes),
                compiler_params=pltpu.CompilerParams(vmem_limit_bytes=vmem_room(held)),
                cost_estimate=cost(2 * panel * items * (part + out), 2 * items * (part + out)),
                name="pairs_own" if own else "pairs_far",
            )(block_mask, here, *t_all, *s_all)
        return pl.pallas_call(
            functools.partial(pair_kernel, planes, lanes, rows, out, width, own),
            out_shape=shapes,
            in_specs=[SMEM, SMEM] + [ANY] * (pieces + 2 * lanes),
            out_specs=[VMEM] * len(shapes),
            scratch_shapes=[
                pltpu.VMEM((items, part), jnp.bfloat16),
                pltpu.VMEM((items, out), jnp.bfloat16),
                pltpu.VMEM((pieces * EXTRA, out), jnp.bfloat16),
                pltpu.VMEM((8, items), jnp.float32),
                pltpu.VMEM((panel, 128), jnp.float32),
                pltpu.VMEM((panel, out), jnp.float32),
                pltpu.SemaphoreType.DMA((pieces,)),
                pltpu.SemaphoreType.DMA((pieces,)),
                pltpu.SemaphoreType.DMA((pieces,)),
            ],
            compiler_params=pltpu.CompilerParams(vmem_limit_bytes=vmem_room(held)),
            cost_estimate=cost(2 * panel * items * (part + out), 2 * items * (part + out)),
            name="pairs_own" if own else "pairs_far",
        )(block_mask, here, *t_all, *s_all)

    (far_sum,) = pairs(False)
    far_sum = swapped(far_sum, "narrow", FAR)
    own_sum, t_keep = pairs(True)
    sums = own_sum + far_sum.astype(jnp.float32)
    t_keep = pl.pallas_call(
        flip_kernel,
        out_shape=jax.ShapeDtypeStruct((keep, items), jnp.bfloat16),
        in_specs=[VMEM],
        out_specs=VMEM,
        compiler_params=pltpu.CompilerParams(vmem_limit_bytes=vmem_room(4 * items * keep)),
        cost_estimate=cost(0, 4 * items * keep),
        name="flip",
    )(t_keep)

    grad = after(sums[:rows], t_keep)
    for k in range(1, planes):
        piece = sums[k * rows : (k + 1) * rows].astype(jnp.bfloat16)
        grad = grad + swapped(piece, "wide", k).astype(jnp.float32)
    coef = 2.0 * width / (items * out)
    grad = (grad * coef).astype(jnp.bfloat16)
    g_parts = [swapped(grad, "wide", k) for k in range(1, planes)]
    g_near = jnp.concatenate([grad, swapped(grad, "narrow", FAR)], 0)
    g_rest = after(jnp.concatenate(g_parts, 0), g_near)
    g_rest = jnp.concatenate([g_rest, swapped(g_rest, "narrow", FAR)], 0)
    g_all = [g_near, swapped(g_near, "narrow", CORE), g_rest, swapped(g_rest, "narrow", CORE)]
    return pl.pallas_call(
        functools.partial(last_kernel, planes, lanes, rows),
        out_shape=jax.ShapeDtypeStruct((keep, out), jnp.float32),
        in_specs=[VMEM] * 5,
        out_specs=VMEM,
        compiler_params=pltpu.CompilerParams(vmem_limit_bytes=vmem_room(4 * items * (out + keep))),
        cost_estimate=cost(2 * items * keep * out, 2 * items * (keep + out)),
        name="last",
    )(t_keep, *g_all)


def solution(mesh):
    in_specs = (
        P(("parts", "wide", "narrow"), None),
        P(),
        P("parts", None),
        P(("parts", "wide", "narrow")),
    )
    out_specs = P(("parts", "wide", "narrow"), None)
    return jax.shard_map(
        per_device, mesh=mesh, in_specs=in_specs, out_specs=out_specs, check_vma=False
    )
```

```python
import functools

import jax
import jax.numpy as jnp
from jax import lax
from jax.experimental import pallas as pl
from jax.experimental.pallas import tpu as pltpu
from jax.sharding import PartitionSpec as P

ANY = pl.BlockSpec(memory_space=pl.ANY)
VMEM = pl.BlockSpec(memory_space=pltpu.VMEM)
SMEM = pl.BlockSpec(memory_space=pltpu.SMEM)
MIB = 1024 * 1024
EXTRA = 16
FAR, CORE = 2, 1
HELD = 72_000_000
NEAR = 2


def swapped(value, axis, bit):
    count = lax.axis_size(axis)
    return lax.ppermute(value, axis, [(source, source ^ bit) for source in range(count)])


def after(value, *others):
    return lax.optimization_barrier((value, *others))[0]


def vmem_room(held):
    return held + 14 * MIB


def cost(flops, moved):
    return pl.CostEstimate(flops=flops, bytes_accessed=moved, transcendentals=0)


def nt(a, b):
    return lax.dot_general(a, b, (((1,), (1,)), ((), ())), preferred_element_type=jnp.float32)


def loop(count, body):
    if count <= 4:
        for step in range(count):
            body(step)
    else:
        lax.fori_loop(0, count, lambda step, carry: (body(step), carry)[1], 0)


def student_kernel(steps, teacher, weight, group, packed, t_all, w_all, t_sem, w_sem):
    rows, width = teacher.shape
    out = weight.shape[1]
    depth = width // steps

    def w_copy(step):
        part = pl.ds(step * depth, depth)
        return pltpu.make_async_copy(weight.at[part], w_all.at[part], w_sem.at[step])

    def t_copy(step):
        part = pl.ds(step * depth, depth)
        return pltpu.make_async_copy(teacher.at[:, part], t_all.at[:, part], t_sem.at[step])

    for step in range(steps):
        t_copy(step).start()
        w_copy(step).start()
    line = jnp.broadcast_to(group[...].astype(jnp.float32), (EXTRA, rows))
    packed[rows:, :rows] = line.astype(jnp.bfloat16)
    total = jnp.zeros((rows, out), jnp.float32)
    for step in range(steps):
        t_copy(step).wait()
        w_copy(step).wait()
        total += jnp.dot(
            t_all[:, step * depth : (step + 1) * depth],
            w_all[step * depth : (step + 1) * depth, :].astype(jnp.bfloat16),
            preferred_element_type=jnp.float32,
        )
    packed[:rows, :] = total.astype(jnp.bfloat16)


def pair_kernel(planes, lanes, rows, out, width, own, mask, place, *refs):
    pieces = planes * lanes
    panel = planes * rows
    prow = rows + EXTRA
    t_in, s_in = refs[:pieces], refs[pieces : pieces + 2 * lanes]
    result = refs[pieces + 2 * lanes]
    rest = list(refs[pieces + 2 * lanes + 1 :])
    t_keep = rest.pop(0) if own else None
    t_all, s_all, g_raw, g_row, g_col, total, t_sem, s_sem, g_sem = rest
    here = place[0]
    lead = 0 if own else FAR

    def t_copy(m, k):
        at = m * planes + k
        return pltpu.make_async_copy(t_in[at], t_all.at[pl.ds(at * rows, rows)], t_sem.at[at])

    def s_part(m, k, first, count):
        late = k >= NEAR
        return s_in[2 * m + late].at[pl.ds((k - late * NEAR) * prow + first, count)]

    def s_copy(m, k):
        at = m * planes + k
        return pltpu.make_async_copy(
            s_part(m, k, 0, rows), s_all.at[pl.ds(at * rows, rows)], s_sem.at[at]
        )

    def g_copy(m, k):
        at = m * planes + k
        return pltpu.make_async_copy(
            s_part(m, k, rows, EXTRA),
            g_raw.at[pl.ds(at * EXTRA, EXTRA)],
            g_sem.at[at],
        )

    order = [lead] + [m for m in range(lanes) if m != lead]
    for m in order:
        for k in range(planes):
            for copy in (g_copy(m, k), t_copy(m, k), s_copy(m, k)):
                copy.start()
    for m in order:
        for k in range(planes):
            at = m * planes + k
            g_copy(m, k).wait()
            line = g_raw[at * EXTRA : (at + 1) * EXTRA, :rows].astype(jnp.float32)[:1]
            g_row[:, at * rows : (at + 1) * rows] = jnp.broadcast_to(line, (8, rows))
            if m == lead:
                g_col[k * rows : (k + 1) * rows, :] = jnp.broadcast_to(line, (128, rows)).T
    total[...] = jnp.zeros_like(total)
    side = min(panel, 512)
    steps = panel // side
    group = side // rows

    for m in order:
        for k in range(planes):
            t_copy(m, k).wait()
            s_copy(m, k).wait()

        def one_row(it, m=m):
            at_i = pl.multiple_of(it * side, side)
            rows_t = t_all[pl.ds(lead * panel + at_i, side), :]
            col = g_col[pl.ds(at_i, side), :]

            def one_tile(jt):
                at_j = pl.multiple_of(m * panel + jt * side, side)
                teach = nt(rows_t, t_all[pl.ds(at_j, side), :]) * (-1.0 / width)
                students = s_all[pl.ds(at_j, side), :]
                line = g_row[:1, pl.ds(at_j, side)]
                same = jnp.concatenate([col] * (side // 128), 1) == line
                terms = []
                for k in range(group):
                    mine = here ^ (it * group + k)
                    weights = []
                    for other in range(group):
                        theirs = here ^ (jt * group + other)
                        both = mask[mine, theirs] + mask[theirs, mine]
                        weights.append(jnp.full((1, rows), both.astype(jnp.float32)))
                    weight = jnp.concatenate(weights, 1)
                    factor = jnp.where(same[k * rows : (k + 1) * rows], 2.0 * weight, weight)
                    error = teach[k * rows : (k + 1) * rows]
                    if own and k == 0:
                        stud = nt(s_all[:rows, :], students) * (1.0 / out)
                        if steps > 1:
                            stud = jnp.where(it == 0, stud, 0.0)
                        error = error + stud
                    terms.append((factor * error).astype(jnp.bfloat16))
                term = jnp.concatenate(terms, 0)
                total[pl.ds(at_i, side), :] += jnp.dot(
                    term, students, preferred_element_type=jnp.float32
                )

            loop(steps, one_tile)

        loop(steps, one_row)
    result[...] = total[...].astype(result.dtype)
    if own:
        keep = t_keep.shape[1]
        for c in range(2):

            @pl.when(place[1] % 2 == c)
            def _(c=c):
                t_keep[...] = t_all[:, c * keep : (c + 1) * keep]


def pair_values_kernel(planes, lanes, rows, out, width, own, chosen, mask, place, *refs):
    pieces = planes * lanes
    prow = rows + EXTRA
    t_in, s_in = refs[:pieces], refs[pieces : pieces + 2 * lanes]
    result = refs[pieces + 2 * lanes]
    here = place[0]
    lead = 0 if own else FAR

    def joined(parts, axis=0):
        return jnp.concatenate(list(parts), axis)

    def panel_of(m, some=range(planes)):
        return joined(t_in[m * planes + k][...] for k in some)

    def s_part(m, k, first, count):
        late = k >= NEAR
        at = (k - late * NEAR) * prow + first
        return s_in[2 * m + late][at : at + count, :]

    def students_of(m):
        return joined(s_part(m, k, 0, rows) for k in range(planes))

    def groups_of(m, k):
        return s_part(m, k, rows, EXTRA)[:, :rows].astype(jnp.float32)[:1]

    weights = []
    for k in chosen:
        scalars = [mask[here ^ k, here ^ j] + mask[here ^ j, here ^ k] for j in range(planes)]
        line = [jnp.full((1, rows), one.astype(jnp.float32) * (-1.0 / width)) for one in scalars]
        weights.append(joined(line, 1))
    column = joined(jnp.broadcast_to(groups_of(lead, k), (128, rows)).T for k in chosen)
    column = joined([column] * (planes * rows // 128), 1)
    lead_t = panel_of(lead, chosen)
    total = jnp.zeros((len(chosen) * rows, out), jnp.float32)
    for m in [lead] + [m for m in range(lanes) if m != lead]:
        students = students_of(m)
        teach = nt(lead_t, panel_of(m))
        same = column == joined((groups_of(m, k) for k in range(planes)), 1)
        terms = []
        for place_at, k in enumerate(chosen):
            span = slice(place_at * rows, (place_at + 1) * rows)
            weight = weights[place_at]
            error = teach[span]
            if own and k == 0:
                error = error - nt(s_in[0][:rows, :], students) * (width / out)
            factor = jnp.where(same[span], 2.0 * weight, weight)
            terms.append((factor * error).astype(jnp.bfloat16))
        total = total + jnp.dot(joined(terms), students, preferred_element_type=jnp.float32)
    result[...] = total.astype(result.dtype)
    if own:
        t_keep = refs[pieces + 2 * lanes + 1]
        keep = t_keep.shape[1]
        for c in range(2):

            @pl.when(place[1] % 2 == c)
            def _(c=c):
                for at in range(pieces):
                    t_keep[at * rows : (at + 1) * rows, :] = t_in[at][:, c * keep : (c + 1) * keep]


def hold_kernel(*refs):
    half = len(refs) // 2
    for source, target in zip(refs[:half], refs[half:]):
        target[...] = source[...]


def flip_kernel(value, result):
    result[...] = value[...].T


def last_kernel(planes, lanes, rows, t_keep, *refs):
    g_in, result = refs[:4], refs[4]
    total = None
    for at in range(4):
        count = 1 if at < 2 else planes - 1
        for far in range(lanes // 2):
            first = (2 * far + at % 2) * planes + (at >= 2)
            one = jnp.dot(
                t_keep[:, first * rows : (first + count) * rows],
                g_in[at][far * count * rows : (far + 1) * count * rows, :],
                preferred_element_type=jnp.float32,
            )
            total = one if total is None else total + one
    result[...] = total


def per_device(teacher, weight, block_mask, item_group):
    rows, width = teacher.shape
    out = weight.shape[1]
    planes = lax.axis_size("wide")
    lanes = lax.axis_size("narrow")
    plane = lax.axis_index("wide")
    lane = lax.axis_index("narrow")
    cols = width // planes
    part = cols // 2
    keep = cols // lanes
    items = rows * planes * lanes
    panel = rows * planes
    pieces = planes * lanes
    here = jnp.stack([plane, lane]).astype(jnp.int32)
    half = planes // 2

    def cut(k, side):
        start = (plane ^ k) * cols + (lane // 2 ^ side) * part
        return lax.dynamic_slice_in_dim(teacher, start, part, 1)

    mine = [cut(k, 0) for k in range(planes)]
    theirs = jnp.concatenate([cut(k, 1) for k in range(planes)], 0)
    got = swapped(theirs, "narrow", FAR)
    got = [got[k * rows : (k + 1) * rows] for k in range(planes)]
    own_core = swapped(mine[0], "narrow", CORE)
    first = [mine[0]] + [swapped(mine[k], "wide", k) for k in range(1, planes)]
    second = [got[0]] + [swapped(got[k], "wide", k) for k in range(1, planes)]

    steps = 8
    packed = pl.pallas_call(
        functools.partial(student_kernel, steps),
        out_shape=jax.ShapeDtypeStruct((rows + EXTRA, out), jnp.bfloat16),
        in_specs=[ANY, ANY, VMEM],
        out_specs=VMEM,
        scratch_shapes=[
            pltpu.VMEM((rows, width), jnp.bfloat16),
            pltpu.VMEM((width, out), jnp.float32),
            pltpu.SemaphoreType.DMA((steps,)),
            pltpu.SemaphoreType.DMA((steps,)),
        ],
        compiler_params=pltpu.CompilerParams(vmem_limit_bytes=56 * MIB),
        cost_estimate=cost(2 * rows * width * out, width * (2 * rows + 4 * out)),
        name="student",
    )(after(teacher, own_core), weight, item_group.reshape(1, rows))
    s_of = {0: packed}
    bit = half
    while bit:
        for k in sorted(s_of):
            s_of[k ^ bit] = swapped(s_of[k], "wide", bit)
        bit //= 2
    s_all = [None] * lanes * 2
    for part_at, odd in enumerate((0, 1)):
        own = jnp.concatenate([s_of[k] for k in range(planes) if (k >= NEAR) == odd], 0)
        far = swapped(own, "narrow", FAR)
        for m, value in ((0, own), (FAR, far)):
            s_all[2 * m + part_at] = value
            s_all[2 * (m ^ CORE) + part_at] = swapped(value, "narrow", CORE)

    t_all = [*first, own_core, *(swapped(t, "narrow", CORE) for t in first[1:])]
    t_all += [*second, *(swapped(t, "narrow", CORE) for t in second)]

    late = 2 * planes
    t_all[late:] = pl.pallas_call(
        hold_kernel,
        out_shape=[jax.ShapeDtypeStruct((rows, part), jnp.bfloat16)] * late,
        in_specs=[VMEM] * late,
        out_specs=[VMEM] * late,
        compiler_params=pltpu.CompilerParams(vmem_limit_bytes=vmem_room(8 * late * rows * part)),
        cost_estimate=cost(0, HELD),
        name="hold",
    )(*t_all[late:])

    whole_tiles = pieces <= 16 and panel <= 512

    def pairs(own, chosen):
        chosen = tuple(chosen)
        some = len(chosen) * rows
        shapes = [jax.ShapeDtypeStruct((some, out), jnp.float32 if own else jnp.bfloat16)]
        if own:
            shapes.append(jax.ShapeDtypeStruct((items, keep), jnp.bfloat16))
        held = items * (2 * part + 2 * out) + 4 * panel * out
        if whole_tiles:
            return pl.pallas_call(
                functools.partial(pair_values_kernel, planes, lanes, rows, out, width, own, chosen),
                out_shape=shapes,
                in_specs=[SMEM, SMEM] + [VMEM] * (pieces + 2 * lanes),
                out_specs=[VMEM] * len(shapes),
                compiler_params=pltpu.CompilerParams(vmem_limit_bytes=vmem_room(held)),
                cost_estimate=cost(2 * some * items * (part + out), 2 * items * (part + out)),
                name="pairs_own" if own else "pairs_far",
            )(block_mask, here, *t_all, *s_all)
        return pl.pallas_call(
            functools.partial(pair_kernel, planes, lanes, rows, out, width, own),
            out_shape=shapes,
            in_specs=[SMEM, SMEM] + [ANY] * (pieces + 2 * lanes),
            out_specs=[VMEM] * len(shapes),
            scratch_shapes=[
                pltpu.VMEM((items, part), jnp.bfloat16),
                pltpu.VMEM((items, out), jnp.bfloat16),
                pltpu.VMEM((pieces * EXTRA, out), jnp.bfloat16),
                pltpu.VMEM((8, items), jnp.float32),
                pltpu.VMEM((panel, 128), jnp.float32),
                pltpu.VMEM((panel, out), jnp.float32),
                pltpu.SemaphoreType.DMA((pieces,)),
                pltpu.SemaphoreType.DMA((pieces,)),
                pltpu.SemaphoreType.DMA((pieces,)),
            ],
            compiler_params=pltpu.CompilerParams(vmem_limit_bytes=vmem_room(held)),
            cost_estimate=cost(2 * panel * items * (part + out), 2 * items * (part + out)),
            name="pairs_own" if own else "pairs_far",
        )(block_mask, here, *t_all, *s_all)

    if whole_tiles:
        (far_high,) = pairs(False, range(half, planes))
        far_high = swapped(far_high, "narrow", FAR)
        (far_low,) = pairs(False, range(half))
        far_low = swapped(far_low, "narrow", FAR)
    else:
        (far_all,) = pairs(False, range(planes))
        far_high = swapped(far_all[half * rows :], "narrow", FAR)
        far_low = swapped(far_all[: half * rows], "narrow", FAR)
    own_sum, t_keep = pairs(True, range(planes))
    sums_high = own_sum[half * rows :] + far_high.astype(jnp.float32)
    sums_low = own_sum[: half * rows] + far_low.astype(jnp.float32)
    t_keep = pl.pallas_call(
        flip_kernel,
        out_shape=jax.ShapeDtypeStruct((keep, items), jnp.bfloat16),
        in_specs=[VMEM],
        out_specs=VMEM,
        compiler_params=pltpu.CompilerParams(vmem_limit_bytes=vmem_room(4 * items * keep)),
        cost_estimate=cost(0, 4 * items * keep),
        name="flip",
    )(t_keep)

    grad = after(sums_low[:rows], t_keep)
    for k in range(1, planes):
        at = k % half * rows
        piece = (sums_low, sums_high)[k >= half][at : at + rows].astype(jnp.bfloat16)
        grad = grad + swapped(piece, "wide", k).astype(jnp.float32)
    coef = 2.0 * width / (items * out)
    grad = (grad * coef).astype(jnp.bfloat16)
    g_parts = [swapped(grad, "wide", k) for k in range(1, planes)]
    g_near = jnp.concatenate([grad, swapped(grad, "narrow", FAR)], 0)
    g_rest = after(jnp.concatenate(g_parts, 0), g_near)
    g_rest = jnp.concatenate([g_rest, swapped(g_rest, "narrow", FAR)], 0)
    g_all = [g_near, swapped(g_near, "narrow", CORE), g_rest, swapped(g_rest, "narrow", CORE)]
    return pl.pallas_call(
        functools.partial(last_kernel, planes, lanes, rows),
        out_shape=jax.ShapeDtypeStruct((keep, out), jnp.float32),
        in_specs=[VMEM] * 5,
        out_specs=VMEM,
        compiler_params=pltpu.CompilerParams(vmem_limit_bytes=vmem_room(4 * items * (out + keep))),
        cost_estimate=cost(2 * items * keep * out, 2 * items * (keep + out)),
        name="last",
    )(t_keep, *g_all)


def solution(mesh):
    in_specs = (
        P(("parts", "wide", "narrow"), None),
        P(),
        P("parts", None),
        P(("parts", "wide", "narrow")),
    )
    out_specs = P(("parts", "wide", "narrow"), None)
    return jax.shard_map(
        per_device, mesh=mesh, in_specs=in_specs, out_specs=out_specs, check_vma=False
    )
```

```python
import functools

import jax
import jax.numpy as jnp
from jax import lax
from jax.experimental import pallas as pl
from jax.experimental.pallas import tpu as pltpu
from jax.sharding import PartitionSpec as P

ANY = pl.BlockSpec(memory_space=pl.ANY)
VMEM = pl.BlockSpec(memory_space=pltpu.VMEM)
SMEM = pl.BlockSpec(memory_space=pltpu.SMEM)
MIB = 1024 * 1024
EXTRA = 16
FAR, CORE = 2, 1
HELD = 72_000_000
NEAR = 2


def swapped(value, axis, bit):
    count = lax.axis_size(axis)
    return lax.ppermute(value, axis, [(source, source ^ bit) for source in range(count)])


def after(value, *others):
    return lax.optimization_barrier((value, *others))[0]


def vmem_room(held):
    return held + 14 * MIB


def cost(flops, moved):
    return pl.CostEstimate(flops=flops, bytes_accessed=moved, transcendentals=0)


def nt(a, b):
    return lax.dot_general(a, b, (((1,), (1,)), ((), ())), preferred_element_type=jnp.float32)


def loop(count, body):
    if count <= 4:
        for step in range(count):
            body(step)
    else:
        lax.fori_loop(0, count, lambda step, carry: (body(step), carry)[1], 0)


def student_kernel(steps, teacher, weight, group, packed, t_all, w_all, t_sem, w_sem):
    rows, width = teacher.shape
    out = weight.shape[1]
    depth = width // steps

    def w_copy(step):
        part = pl.ds(step * depth, depth)
        return pltpu.make_async_copy(weight.at[part], w_all.at[part], w_sem.at[step])

    def t_copy(step):
        part = pl.ds(step * depth, depth)
        return pltpu.make_async_copy(teacher.at[:, part], t_all.at[:, part], t_sem.at[step])

    for step in range(steps):
        t_copy(step).start()
        w_copy(step).start()
    line = jnp.broadcast_to(group[...].astype(jnp.float32), (EXTRA, rows))
    packed[rows:, :rows] = line.astype(jnp.bfloat16)
    total = jnp.zeros((rows, out), jnp.float32)
    for step in range(steps):
        t_copy(step).wait()
        w_copy(step).wait()
        total += jnp.dot(
            t_all[:, step * depth : (step + 1) * depth],
            w_all[step * depth : (step + 1) * depth, :].astype(jnp.bfloat16),
            preferred_element_type=jnp.float32,
        )
    packed[:rows, :] = total.astype(jnp.bfloat16)


def pair_kernel(planes, lanes, rows, out, width, own, mask, place, *refs):
    pieces = planes * lanes
    panel = planes * rows
    prow = rows + EXTRA
    t_in, s_in = refs[:pieces], refs[pieces : pieces + 2 * lanes]
    result = refs[pieces + 2 * lanes]
    rest = list(refs[pieces + 2 * lanes + 1 :])
    t_keep = rest.pop(0) if own else None
    t_all, s_all, g_raw, g_row, g_col, total, t_sem, s_sem, g_sem = rest
    here = place[0]
    lead = 0 if own else FAR

    def t_copy(m, k):
        at = m * planes + k
        return pltpu.make_async_copy(t_in[at], t_all.at[pl.ds(at * rows, rows)], t_sem.at[at])

    def s_part(m, k, first, count):
        late = k >= NEAR
        return s_in[2 * m + late].at[pl.ds((k - late * NEAR) * prow + first, count)]

    def s_copy(m, k):
        at = m * planes + k
        return pltpu.make_async_copy(
            s_part(m, k, 0, rows), s_all.at[pl.ds(at * rows, rows)], s_sem.at[at]
        )

    def g_copy(m, k):
        at = m * planes + k
        return pltpu.make_async_copy(
            s_part(m, k, rows, EXTRA),
            g_raw.at[pl.ds(at * EXTRA, EXTRA)],
            g_sem.at[at],
        )

    order = [lead] + [m for m in range(lanes) if m != lead]
    for m in order:
        for k in range(planes):
            for copy in (g_copy(m, k), t_copy(m, k), s_copy(m, k)):
                copy.start()
    for m in order:
        for k in range(planes):
            at = m * planes + k
            g_copy(m, k).wait()
            line = g_raw[at * EXTRA : (at + 1) * EXTRA, :rows].astype(jnp.float32)[:1]
            g_row[:, at * rows : (at + 1) * rows] = jnp.broadcast_to(line, (8, rows))
            if m == lead:
                g_col[k * rows : (k + 1) * rows, :] = jnp.broadcast_to(line, (128, rows)).T
    total[...] = jnp.zeros_like(total)
    side = min(panel, 512)
    steps = panel // side
    group = side // rows

    for m in order:
        for k in range(planes):
            t_copy(m, k).wait()
            s_copy(m, k).wait()

        def one_row(it, m=m):
            at_i = pl.multiple_of(it * side, side)
            rows_t = t_all[pl.ds(lead * panel + at_i, side), :]
            col = g_col[pl.ds(at_i, side), :]

            def one_tile(jt):
                at_j = pl.multiple_of(m * panel + jt * side, side)
                teach = nt(rows_t, t_all[pl.ds(at_j, side), :]) * (-1.0 / width)
                students = s_all[pl.ds(at_j, side), :]
                line = g_row[:1, pl.ds(at_j, side)]
                same = jnp.concatenate([col] * (side // 128), 1) == line
                terms = []
                for k in range(group):
                    mine = here ^ (it * group + k)
                    weights = []
                    for other in range(group):
                        theirs = here ^ (jt * group + other)
                        both = mask[mine, theirs] + mask[theirs, mine]
                        weights.append(jnp.full((1, rows), both.astype(jnp.float32)))
                    weight = jnp.concatenate(weights, 1)
                    factor = jnp.where(same[k * rows : (k + 1) * rows], 2.0 * weight, weight)
                    error = teach[k * rows : (k + 1) * rows]
                    if own and k == 0:
                        stud = nt(s_all[:rows, :], students) * (1.0 / out)
                        if steps > 1:
                            stud = jnp.where(it == 0, stud, 0.0)
                        error = error + stud
                    terms.append((factor * error).astype(jnp.bfloat16))
                term = jnp.concatenate(terms, 0)
                total[pl.ds(at_i, side), :] += jnp.dot(
                    term, students, preferred_element_type=jnp.float32
                )

            loop(steps, one_tile)

        loop(steps, one_row)
    result[...] = total[...].astype(result.dtype)
    if own:
        keep = t_keep.shape[1]
        for c in range(2):

            @pl.when(place[1] % 2 == c)
            def _(c=c):
                t_keep[...] = t_all[:, c * keep : (c + 1) * keep]


def pair_values_kernel(planes, lanes, rows, out, width, own, chosen, mask, place, *refs):
    pieces = planes * lanes
    prow = rows + EXTRA
    t_in, s_in = refs[:pieces], refs[pieces : pieces + 2 * lanes]
    result = refs[pieces + 2 * lanes]
    here = place[0]
    lead = 0 if own else FAR

    def joined(parts, axis=0):
        return jnp.concatenate(list(parts), axis)

    def panel_of(m, some=range(planes)):
        return joined(t_in[m * planes + k][...] for k in some)

    def s_part(m, k, first, count):
        late = k >= NEAR
        at = (k - late * NEAR) * prow + first
        return s_in[2 * m + late][at : at + count, :]

    def students_of(m):
        return joined(s_part(m, k, 0, rows) for k in range(planes))

    def groups_of(m, k):
        return s_part(m, k, rows, EXTRA)[:, :rows].astype(jnp.float32)[:1]

    weights = []
    for k in chosen:
        scalars = [mask[here ^ k, here ^ j] + mask[here ^ j, here ^ k] for j in range(planes)]
        line = [jnp.full((1, rows), one.astype(jnp.float32) * (-1.0 / width)) for one in scalars]
        weights.append(joined(line, 1))
    column = joined(jnp.broadcast_to(groups_of(lead, k), (128, rows)).T for k in chosen)
    column = joined([column] * (planes * rows // 128), 1)
    lead_t = panel_of(lead, chosen)
    total = jnp.zeros((len(chosen) * rows, out), jnp.float32)
    for m in [lead] + [m for m in range(lanes) if m != lead]:
        students = students_of(m)
        teach = nt(lead_t, panel_of(m))
        same = column == joined((groups_of(m, k) for k in range(planes)), 1)
        terms = []
        for place_at, k in enumerate(chosen):
            span = slice(place_at * rows, (place_at + 1) * rows)
            weight = weights[place_at]
            error = teach[span]
            if own and k == 0:
                error = error - nt(s_in[0][:rows, :], students) * (width / out)
            factor = jnp.where(same[span], 2.0 * weight, weight)
            terms.append((factor * error).astype(jnp.bfloat16))
        total = total + jnp.dot(joined(terms), students, preferred_element_type=jnp.float32)
    result[...] = total.astype(result.dtype)
    if own:
        t_keep = refs[pieces + 2 * lanes + 1]
        keep = t_keep.shape[1]
        for c in range(2):

            @pl.when(place[1] % 2 == c)
            def _(c=c):
                for at in range(pieces):
                    t_keep[at * rows : (at + 1) * rows, :] = t_in[at][:, c * keep : (c + 1) * keep]


def hold_kernel(*refs):
    half = len(refs) // 2
    for source, target in zip(refs[:half], refs[half:]):
        target[...] = source[...]


def flip_kernel(value, result):
    result[...] = value[...].T


def last_kernel(planes, lanes, rows, t_keep, *refs):
    g_in, result = refs[:4], refs[4]
    total = None
    for at in range(4):
        count = NEAR if at < 2 else planes - NEAR
        for far in range(lanes // 2):
            first = (2 * far + at % 2) * planes + (at >= 2) * NEAR
            one = jnp.dot(
                t_keep[:, first * rows : (first + count) * rows],
                g_in[at][far * count * rows : (far + 1) * count * rows, :],
                preferred_element_type=jnp.float32,
            )
            total = one if total is None else total + one
    result[...] = total


def per_device(teacher, weight, block_mask, item_group):
    rows, width = teacher.shape
    out = weight.shape[1]
    planes = lax.axis_size("wide")
    lanes = lax.axis_size("narrow")
    plane = lax.axis_index("wide")
    lane = lax.axis_index("narrow")
    cols = width // planes
    part = cols // 2
    keep = cols // lanes
    items = rows * planes * lanes
    panel = rows * planes
    pieces = planes * lanes
    here = jnp.stack([plane, lane]).astype(jnp.int32)
    half = planes // 2

    def cut(k, side):
        start = (plane ^ k) * cols + (lane // 2 ^ side) * part
        return lax.dynamic_slice_in_dim(teacher, start, part, 1)

    mine = [cut(k, 0) for k in range(planes)]
    theirs = jnp.concatenate([cut(k, 1) for k in range(planes)], 0)
    got = swapped(theirs, "narrow", FAR)
    got = [got[k * rows : (k + 1) * rows] for k in range(planes)]
    own_core = swapped(mine[0], "narrow", CORE)
    first = [mine[0]] + [swapped(mine[k], "wide", k) for k in range(1, planes)]
    second = [got[0]] + [swapped(got[k], "wide", k) for k in range(1, planes)]

    steps = 8
    packed = pl.pallas_call(
        functools.partial(student_kernel, steps),
        out_shape=jax.ShapeDtypeStruct((rows + EXTRA, out), jnp.bfloat16),
        in_specs=[ANY, ANY, VMEM],
        out_specs=VMEM,
        scratch_shapes=[
            pltpu.VMEM((rows, width), jnp.bfloat16),
            pltpu.VMEM((width, out), jnp.float32),
            pltpu.SemaphoreType.DMA((steps,)),
            pltpu.SemaphoreType.DMA((steps,)),
        ],
        compiler_params=pltpu.CompilerParams(vmem_limit_bytes=56 * MIB),
        cost_estimate=cost(2 * rows * width * out, width * (2 * rows + 4 * out)),
        name="student",
    )(after(teacher, own_core), weight, item_group.reshape(1, rows))
    s_of = {0: packed}
    bit = half
    while bit:
        for k in sorted(s_of):
            s_of[k ^ bit] = swapped(s_of[k], "wide", bit)
        bit //= 2
    s_all = [None] * lanes * 2
    for part_at, odd in enumerate((0, 1)):
        own = jnp.concatenate([s_of[k] for k in range(planes) if (k >= NEAR) == odd], 0)
        far = swapped(own, "narrow", FAR)
        for m, value in ((0, own), (FAR, far)):
            s_all[2 * m + part_at] = value
            s_all[2 * (m ^ CORE) + part_at] = swapped(value, "narrow", CORE)

    t_all = [*first, own_core, *(swapped(t, "narrow", CORE) for t in first[1:])]
    t_all += [*second, *(swapped(t, "narrow", CORE) for t in second)]

    late = 2 * planes
    t_all[late:] = pl.pallas_call(
        hold_kernel,
        out_shape=[jax.ShapeDtypeStruct((rows, part), jnp.bfloat16)] * late,
        in_specs=[VMEM] * late,
        out_specs=[VMEM] * late,
        compiler_params=pltpu.CompilerParams(vmem_limit_bytes=vmem_room(8 * late * rows * part)),
        cost_estimate=cost(0, HELD),
        name="hold",
    )(*t_all[late:])

    whole_tiles = pieces <= 16 and panel <= 512

    def pairs(own, chosen):
        chosen = tuple(chosen)
        some = len(chosen) * rows
        shapes = [jax.ShapeDtypeStruct((some, out), jnp.float32 if own else jnp.bfloat16)]
        if own:
            shapes.append(jax.ShapeDtypeStruct((items, keep), jnp.bfloat16))
        held = items * (2 * part + 2 * out) + 4 * panel * out
        if whole_tiles:
            return pl.pallas_call(
                functools.partial(pair_values_kernel, planes, lanes, rows, out, width, own, chosen),
                out_shape=shapes,
                in_specs=[SMEM, SMEM] + [VMEM] * (pieces + 2 * lanes),
                out_specs=[VMEM] * len(shapes),
                compiler_params=pltpu.CompilerParams(vmem_limit_bytes=vmem_room(held)),
                cost_estimate=cost(2 * some * items * (part + out), 2 * items * (part + out)),
                name="pairs_own" if own else "pairs_far",
            )(block_mask, here, *t_all, *s_all)
        return pl.pallas_call(
            functools.partial(pair_kernel, planes, lanes, rows, out, width, own),
            out_shape=shapes,
            in_specs=[SMEM, SMEM] + [ANY] * (pieces + 2 * lanes),
            out_specs=[VMEM] * len(shapes),
            scratch_shapes=[
                pltpu.VMEM((items, part), jnp.bfloat16),
                pltpu.VMEM((items, out), jnp.bfloat16),
                pltpu.VMEM((pieces * EXTRA, out), jnp.bfloat16),
                pltpu.VMEM((8, items), jnp.float32),
                pltpu.VMEM((panel, 128), jnp.float32),
                pltpu.VMEM((panel, out), jnp.float32),
                pltpu.SemaphoreType.DMA((pieces,)),
                pltpu.SemaphoreType.DMA((pieces,)),
                pltpu.SemaphoreType.DMA((pieces,)),
            ],
            compiler_params=pltpu.CompilerParams(vmem_limit_bytes=vmem_room(held)),
            cost_estimate=cost(2 * panel * items * (part + out), 2 * items * (part + out)),
            name="pairs_own" if own else "pairs_far",
        )(block_mask, here, *t_all, *s_all)

    if whole_tiles:
        (far_high,) = pairs(False, range(half, planes))
        far_high = swapped(far_high, "narrow", FAR)
        (far_low,) = pairs(False, range(half))
        far_low = swapped(far_low, "narrow", FAR)
    else:
        (far_all,) = pairs(False, range(planes))
        far_high = swapped(far_all[half * rows :], "narrow", FAR)
        far_low = swapped(far_all[: half * rows], "narrow", FAR)
    own_sum, t_keep = pairs(True, range(planes))
    sums_high = own_sum[half * rows :] + far_high.astype(jnp.float32)
    sums_low = own_sum[: half * rows] + far_low.astype(jnp.float32)
    t_keep = pl.pallas_call(
        flip_kernel,
        out_shape=jax.ShapeDtypeStruct((keep, items), jnp.bfloat16),
        in_specs=[VMEM],
        out_specs=VMEM,
        compiler_params=pltpu.CompilerParams(vmem_limit_bytes=vmem_room(4 * items * keep)),
        cost_estimate=cost(0, 4 * items * keep),
        name="flip",
    )(t_keep)

    grad = after(sums_low[:rows], t_keep)
    for k in range(1, planes):
        at = k % half * rows
        piece = (sums_low, sums_high)[k >= half][at : at + rows].astype(jnp.bfloat16)
        grad = grad + swapped(piece, "wide", k).astype(jnp.float32)
    coef = 2.0 * width / (items * out)
    grad = (grad * coef).astype(jnp.bfloat16)
    g_parts = [swapped(grad, "wide", k) for k in range(1, planes)]
    g_near = jnp.concatenate([grad, *g_parts[: NEAR - 1]], 0)
    g_near = jnp.concatenate([g_near, swapped(g_near, "narrow", FAR)], 0)
    g_rest = jnp.concatenate(g_parts[NEAR - 1 :], 0)
    g_rest = jnp.concatenate([g_rest, swapped(g_rest, "narrow", FAR)], 0)
    g_all = [g_near, swapped(g_near, "narrow", CORE), g_rest, swapped(g_rest, "narrow", CORE)]
    return pl.pallas_call(
        functools.partial(last_kernel, planes, lanes, rows),
        out_shape=jax.ShapeDtypeStruct((keep, out), jnp.float32),
        in_specs=[VMEM] * 5,
        out_specs=VMEM,
        compiler_params=pltpu.CompilerParams(vmem_limit_bytes=vmem_room(4 * items * (out + keep))),
        cost_estimate=cost(2 * items * keep * out, 2 * items * (keep + out)),
        name="last",
    )(t_keep, *g_all)


def solution(mesh):
    in_specs = (
        P(("parts", "wide", "narrow"), None),
        P(),
        P("parts", None),
        P(("parts", "wide", "narrow")),
    )
    out_specs = P(("parts", "wide", "narrow"), None)
    return jax.shard_map(
        per_device, mesh=mesh, in_specs=in_specs, out_specs=out_specs, check_vma=False
    )
```

```python
import functools

import jax
import jax.numpy as jnp
from jax import lax
from jax.experimental import pallas as pl
from jax.experimental.pallas import tpu as pltpu
from jax.sharding import PartitionSpec as P

ANY = pl.BlockSpec(memory_space=pl.ANY)
VMEM = pl.BlockSpec(memory_space=pltpu.VMEM)
SMEM = pl.BlockSpec(memory_space=pltpu.SMEM)
MIB = 1024 * 1024
EXTRA = 16
FAR, CORE = 2, 1
HELD = 72_000_000
NEAR = 2


def swapped(value, axis, bit):
    count = lax.axis_size(axis)
    return lax.ppermute(value, axis, [(source, source ^ bit) for source in range(count)])


def after(value, *others):
    return lax.optimization_barrier((value, *others))[0]


def vmem_room(held):
    return held + 14 * MIB


def cost(flops, moved):
    return pl.CostEstimate(flops=flops, bytes_accessed=moved, transcendentals=0)


def nt(a, b):
    return lax.dot_general(a, b, (((1,), (1,)), ((), ())), preferred_element_type=jnp.float32)


def loop(count, body):
    if count <= 4:
        for step in range(count):
            body(step)
    else:
        lax.fori_loop(0, count, lambda step, carry: (body(step), carry)[1], 0)


def pair_kernel(planes, lanes, rows, out, width, own, mask, place, *refs):
    pieces = planes * lanes
    panel = planes * rows
    prow = rows + EXTRA
    t_in, s_in = refs[:pieces], refs[pieces : pieces + 2 * lanes]
    result = refs[pieces + 2 * lanes]
    rest = list(refs[pieces + 2 * lanes + 1 :])
    t_keep = rest.pop(0) if own else None
    t_all, s_all, g_raw, g_row, g_col, total, t_sem, s_sem, g_sem = rest
    here = place[0]
    lead = 0 if own else FAR

    def t_copy(m, k):
        at = m * planes + k
        return pltpu.make_async_copy(t_in[at], t_all.at[pl.ds(at * rows, rows)], t_sem.at[at])

    def s_part(m, k, first, count):
        late = k >= NEAR
        return s_in[2 * m + late].at[pl.ds((k - late * NEAR) * prow + first, count)]

    def s_copy(m, k):
        at = m * planes + k
        return pltpu.make_async_copy(
            s_part(m, k, 0, rows), s_all.at[pl.ds(at * rows, rows)], s_sem.at[at]
        )

    def g_copy(m, k):
        at = m * planes + k
        return pltpu.make_async_copy(
            s_part(m, k, rows, EXTRA),
            g_raw.at[pl.ds(at * EXTRA, EXTRA)],
            g_sem.at[at],
        )

    order = [lead] + [m for m in range(lanes) if m != lead]
    for m in order:
        for k in range(planes):
            for copy in (g_copy(m, k), t_copy(m, k), s_copy(m, k)):
                copy.start()
    for m in order:
        for k in range(planes):
            at = m * planes + k
            g_copy(m, k).wait()
            line = g_raw[at * EXTRA : (at + 1) * EXTRA, :rows].astype(jnp.float32)[:1]
            g_row[:, at * rows : (at + 1) * rows] = jnp.broadcast_to(line, (8, rows))
            if m == lead:
                g_col[k * rows : (k + 1) * rows, :] = jnp.broadcast_to(line, (128, rows)).T
    total[...] = jnp.zeros_like(total)
    side = min(panel, 512)
    steps = panel // side
    group = side // rows

    for m in order:
        for k in range(planes):
            t_copy(m, k).wait()
            s_copy(m, k).wait()

        def one_row(it, m=m):
            at_i = pl.multiple_of(it * side, side)
            rows_t = t_all[pl.ds(lead * panel + at_i, side), :]
            col = g_col[pl.ds(at_i, side), :]

            def one_tile(jt):
                at_j = pl.multiple_of(m * panel + jt * side, side)
                teach = nt(rows_t, t_all[pl.ds(at_j, side), :]) * (-1.0 / width)
                students = s_all[pl.ds(at_j, side), :]
                line = g_row[:1, pl.ds(at_j, side)]
                same = jnp.concatenate([col] * (side // 128), 1) == line
                terms = []
                for k in range(group):
                    mine = here ^ (it * group + k)
                    weights = []
                    for other in range(group):
                        theirs = here ^ (jt * group + other)
                        both = mask[mine, theirs] + mask[theirs, mine]
                        weights.append(jnp.full((1, rows), both.astype(jnp.float32)))
                    weight = jnp.concatenate(weights, 1)
                    factor = jnp.where(same[k * rows : (k + 1) * rows], 2.0 * weight, weight)
                    error = teach[k * rows : (k + 1) * rows]
                    if own and k == 0:
                        stud = nt(s_all[:rows, :], students) * (1.0 / out)
                        if steps > 1:
                            stud = jnp.where(it == 0, stud, 0.0)
                        error = error + stud
                    terms.append((factor * error).astype(jnp.bfloat16))
                term = jnp.concatenate(terms, 0)
                total[pl.ds(at_i, side), :] += jnp.dot(
                    term, students, preferred_element_type=jnp.float32
                )

            loop(steps, one_tile)

        loop(steps, one_row)
    result[...] = total[...].astype(result.dtype)
    if own:
        keep = t_keep.shape[1]
        for c in range(2):

            @pl.when(place[1] % 2 == c)
            def _(c=c):
                t_keep[...] = t_all[:, c * keep : (c + 1) * keep]


def pair_values_kernel(planes, lanes, rows, out, width, own, chosen, mask, place, *refs):
    pieces = planes * lanes
    prow = rows + EXTRA
    t_in, s_in = refs[:pieces], refs[pieces : pieces + 2 * lanes]
    result = refs[pieces + 2 * lanes]
    here = place[0]
    lead = 0 if own else FAR

    def joined(parts, axis=0):
        return jnp.concatenate(list(parts), axis)

    def panel_of(m, some=range(planes)):
        return joined(t_in[m * planes + k][...] for k in some)

    def s_part(m, k, first, count):
        late = k >= NEAR
        at = (k - late * NEAR) * prow + first
        return s_in[2 * m + late][at : at + count, :]

    def students_of(m):
        return joined(s_part(m, k, 0, rows) for k in range(planes))

    def groups_of(m, k):
        return s_part(m, k, rows, EXTRA)[:, :rows].astype(jnp.float32)[:1]

    weights = []
    for k in chosen:
        scalars = [mask[here ^ k, here ^ j] + mask[here ^ j, here ^ k] for j in range(planes)]
        line = [jnp.full((1, rows), one.astype(jnp.float32) * (-1.0 / width)) for one in scalars]
        weights.append(joined(line, 1))
    column = joined(jnp.broadcast_to(groups_of(lead, k), (128, rows)).T for k in chosen)
    column = joined([column] * (planes * rows // 128), 1)
    lead_t = panel_of(lead, chosen)
    total = jnp.zeros((len(chosen) * rows, out), jnp.float32)
    for m in [lead] + [m for m in range(lanes) if m != lead]:
        students = students_of(m)
        teach = nt(lead_t, panel_of(m))
        same = column == joined((groups_of(m, k) for k in range(planes)), 1)
        terms = []
        for place_at, k in enumerate(chosen):
            span = slice(place_at * rows, (place_at + 1) * rows)
            weight = weights[place_at]
            error = teach[span]
            if own and k == 0:
                error = error - nt(s_in[0][:rows, :], students) * (width / out)
            factor = jnp.where(same[span], 2.0 * weight, weight)
            terms.append((factor * error).astype(jnp.bfloat16))
        total = total + jnp.dot(joined(terms), students, preferred_element_type=jnp.float32)
    result[...] = total.astype(result.dtype)
    if own:
        t_keep = refs[pieces + 2 * lanes + 1]
        keep = t_keep.shape[1]
        for c in range(2):

            @pl.when(place[1] % 2 == c)
            def _(c=c):
                for at in range(pieces):
                    t_keep[at * rows : (at + 1) * rows, :] = t_in[at][:, c * keep : (c + 1) * keep]


def hold_kernel(*refs):
    half = len(refs) // 2
    for source, target in zip(refs[:half], refs[half:]):
        target[...] = source[...]


def flip_kernel(value, result):
    result[...] = value[...].T


def last_kernel(planes, lanes, rows, t_keep, *refs):
    g_in, result = refs[:4], refs[4]
    total = None
    for at in range(4):
        count = NEAR if at < 2 else planes - NEAR
        for far in range(lanes // 2):
            first = (2 * far + at % 2) * planes + (at >= 2) * NEAR
            one = jnp.dot(
                t_keep[:, first * rows : (first + count) * rows],
                g_in[at][far * count * rows : (far + 1) * count * rows, :],
                preferred_element_type=jnp.float32,
            )
            total = one if total is None else total + one
    result[...] = total


def per_device(teacher, weight, block_mask, item_group):
    rows, width = teacher.shape
    out = weight.shape[1]
    planes = lax.axis_size("wide")
    lanes = lax.axis_size("narrow")
    plane = lax.axis_index("wide")
    lane = lax.axis_index("narrow")
    cols = width // planes
    part = cols // 2
    keep = cols // lanes
    items = rows * planes * lanes
    panel = rows * planes
    pieces = planes * lanes
    here = jnp.stack([plane, lane]).astype(jnp.int32)
    half = planes // 2

    def cut(k, side):
        start = (plane ^ k) * cols + (lane // 2 ^ side) * part
        return lax.dynamic_slice_in_dim(teacher, start, part, 1)

    mine = [cut(k, 0) for k in range(planes)]
    theirs = jnp.concatenate([cut(k, 1) for k in range(planes)], 0)
    got = swapped(theirs, "narrow", FAR)
    got = [got[k * rows : (k + 1) * rows] for k in range(planes)]
    own_core = swapped(mine[0], "narrow", CORE)
    first = [mine[0]] + [swapped(mine[k], "wide", k) for k in range(1, planes)]
    second = [got[0]] + [swapped(got[k], "wide", k) for k in range(1, planes)]

    low_weight = weight.astype(jnp.bfloat16)
    student = jnp.dot(
        after(teacher, own_core), low_weight, preferred_element_type=jnp.float32
    ).astype(jnp.bfloat16)
    extra = jnp.zeros((EXTRA, out), jnp.bfloat16).at[0, :rows].set(item_group.astype(jnp.bfloat16))
    packed = jnp.concatenate([student, extra], 0)

    s_of = {0: packed}
    bit = half
    while bit:
        for k in sorted(s_of):
            s_of[k ^ bit] = swapped(s_of[k], "wide", bit)
        bit //= 2
    s_all = [None] * lanes * 2
    for part_at, odd in enumerate((0, 1)):
        own = jnp.concatenate([s_of[k] for k in range(planes) if (k >= NEAR) == odd], 0)
        far = swapped(own, "narrow", FAR)
        for m, value in ((0, own), (FAR, far)):
            s_all[2 * m + part_at] = value
            s_all[2 * (m ^ CORE) + part_at] = swapped(value, "narrow", CORE)

    t_all = [*first, own_core, *(swapped(t, "narrow", CORE) for t in first[1:])]
    t_all += [*second, *(swapped(t, "narrow", CORE) for t in second)]

    late = 2 * planes
    t_all[late:] = pl.pallas_call(
        hold_kernel,
        out_shape=[jax.ShapeDtypeStruct((rows, part), jnp.bfloat16)] * late,
        in_specs=[VMEM] * late,
        out_specs=[VMEM] * late,
        compiler_params=pltpu.CompilerParams(vmem_limit_bytes=vmem_room(8 * late * rows * part)),
        cost_estimate=cost(0, HELD),
        name="hold",
    )(*t_all[late:])

    whole_tiles = pieces <= 16 and panel <= 512

    def pairs(own, chosen):
        chosen = tuple(chosen)
        some = len(chosen) * rows
        shapes = [jax.ShapeDtypeStruct((some, out), jnp.float32 if own else jnp.bfloat16)]
        if own:
            shapes.append(jax.ShapeDtypeStruct((items, keep), jnp.bfloat16))
        held = items * (2 * part + 2 * out) + 4 * panel * out
        if whole_tiles:
            return pl.pallas_call(
                functools.partial(pair_values_kernel, planes, lanes, rows, out, width, own, chosen),
                out_shape=shapes,
                in_specs=[SMEM, SMEM] + [VMEM] * (pieces + 2 * lanes),
                out_specs=[VMEM] * len(shapes),
                compiler_params=pltpu.CompilerParams(vmem_limit_bytes=vmem_room(held)),
                cost_estimate=cost(2 * some * items * (part + out), 2 * items * (part + out)),
                name="pairs_own" if own else "pairs_far",
            )(block_mask, here, *t_all, *s_all)
        return pl.pallas_call(
            functools.partial(pair_kernel, planes, lanes, rows, out, width, own),
            out_shape=shapes,
            in_specs=[SMEM, SMEM] + [ANY] * (pieces + 2 * lanes),
            out_specs=[VMEM] * len(shapes),
            scratch_shapes=[
                pltpu.VMEM((items, part), jnp.bfloat16),
                pltpu.VMEM((items, out), jnp.bfloat16),
                pltpu.VMEM((pieces * EXTRA, out), jnp.bfloat16),
                pltpu.VMEM((8, items), jnp.float32),
                pltpu.VMEM((panel, 128), jnp.float32),
                pltpu.VMEM((panel, out), jnp.float32),
                pltpu.SemaphoreType.DMA((pieces,)),
                pltpu.SemaphoreType.DMA((pieces,)),
                pltpu.SemaphoreType.DMA((pieces,)),
            ],
            compiler_params=pltpu.CompilerParams(vmem_limit_bytes=vmem_room(held)),
            cost_estimate=cost(2 * panel * items * (part + out), 2 * items * (part + out)),
            name="pairs_own" if own else "pairs_far",
        )(block_mask, here, *t_all, *s_all)

    if whole_tiles:
        (far_high,) = pairs(False, range(1, planes))
        far_high = swapped(far_high, "narrow", FAR)
        (far_low,) = pairs(False, range(1))
        far_low = swapped(far_low, "narrow", FAR)
    else:
        (far_all,) = pairs(False, range(planes))
        far_high = swapped(far_all[rows:], "narrow", FAR)
        far_low = swapped(far_all[:rows], "narrow", FAR)
    own_sum, t_keep = pairs(True, range(planes))
    sums_high = own_sum[rows:] + far_high.astype(jnp.float32)
    sums_low = own_sum[:rows] + far_low.astype(jnp.float32)
    t_keep = pl.pallas_call(
        flip_kernel,
        out_shape=jax.ShapeDtypeStruct((keep, items), jnp.bfloat16),
        in_specs=[VMEM],
        out_specs=VMEM,
        compiler_params=pltpu.CompilerParams(vmem_limit_bytes=vmem_room(4 * items * keep)),
        cost_estimate=cost(0, 4 * items * keep),
        name="flip",
    )(t_keep)

    grad = after(sums_low, t_keep)
    for k in range(1, planes):
        piece = sums_high[(k - 1) * rows : k * rows].astype(jnp.bfloat16)
        grad = grad + swapped(piece, "wide", k).astype(jnp.float32)
    coef = 2.0 * width / (items * out)
    grad = (grad * coef).astype(jnp.bfloat16)
    g_parts = [swapped(grad, "wide", k) for k in range(1, planes)]
    g_near = jnp.concatenate([grad, *g_parts[: NEAR - 1]], 0)
    g_near = jnp.concatenate([g_near, swapped(g_near, "narrow", FAR)], 0)
    g_rest = jnp.concatenate(g_parts[NEAR - 1 :], 0)
    g_rest = jnp.concatenate([g_rest, swapped(g_rest, "narrow", FAR)], 0)
    g_all = [g_near, swapped(g_near, "narrow", CORE), g_rest, swapped(g_rest, "narrow", CORE)]
    return pl.pallas_call(
        functools.partial(last_kernel, planes, lanes, rows),
        out_shape=jax.ShapeDtypeStruct((keep, out), jnp.float32),
        in_specs=[VMEM] * 5,
        out_specs=VMEM,
        compiler_params=pltpu.CompilerParams(vmem_limit_bytes=vmem_room(4 * items * (out + keep))),
        cost_estimate=cost(2 * items * keep * out, 2 * items * (keep + out)),
        name="last",
    )(t_keep, *g_all)


def solution(mesh):
    in_specs = (
        P(("parts", "wide", "narrow"), None),
        P(),
        P("parts", None),
        P(("parts", "wide", "narrow")),
    )
    out_specs = P(("parts", "wide", "narrow"), None)
    return jax.shard_map(
        per_device, mesh=mesh, in_specs=in_specs, out_specs=out_specs, check_vma=False
    )
```

```python
import functools

import jax
import jax.numpy as jnp
from jax import lax
from jax.experimental import pallas as pl
from jax.experimental.pallas import tpu as pltpu
from jax.sharding import PartitionSpec as P

ANY = pl.BlockSpec(memory_space=pl.ANY)
VMEM = pl.BlockSpec(memory_space=pltpu.VMEM)
SMEM = pl.BlockSpec(memory_space=pltpu.SMEM)
MIB = 1024 * 1024
EXTRA = 16
FAR, CORE = 2, 1
HELD = 72_000_000
NEAR = 2


def swapped(value, axis, bit):
    count = lax.axis_size(axis)
    return lax.ppermute(value, axis, [(source, source ^ bit) for source in range(count)])


def after(value, *others):
    return lax.optimization_barrier((value, *others))[0]


def vmem_room(held):
    return held + 14 * MIB


def cost(flops, moved):
    return pl.CostEstimate(flops=flops, bytes_accessed=moved, transcendentals=0)


def nt(a, b):
    return lax.dot_general(a, b, (((1,), (1,)), ((), ())), preferred_element_type=jnp.float32)


def loop(count, body):
    if count <= 4:
        for step in range(count):
            body(step)
    else:
        lax.fori_loop(0, count, lambda step, carry: (body(step), carry)[1], 0)


def pair_kernel(planes, lanes, rows, out, width, own, mask, place, *refs):
    pieces = planes * lanes
    panel = planes * rows
    prow = rows + EXTRA
    t_in, s_in = refs[:pieces], refs[pieces : pieces + 2 * lanes]
    result = refs[pieces + 2 * lanes]
    rest = list(refs[pieces + 2 * lanes + 1 :])
    t_keep = rest.pop(0) if own else None
    t_all, s_all, g_raw, g_row, g_col, total, t_sem, s_sem, g_sem = rest
    here = place[0]
    lead = 0 if own else FAR

    def t_copy(m, k):
        at = m * planes + k
        return pltpu.make_async_copy(t_in[at], t_all.at[pl.ds(at * rows, rows)], t_sem.at[at])

    def s_part(m, k, first, count):
        late = k >= NEAR
        return s_in[2 * m + late].at[pl.ds((k - late * NEAR) * prow + first, count)]

    def s_copy(m, k):
        at = m * planes + k
        return pltpu.make_async_copy(
            s_part(m, k, 0, rows), s_all.at[pl.ds(at * rows, rows)], s_sem.at[at]
        )

    def g_copy(m, k):
        at = m * planes + k
        return pltpu.make_async_copy(
            s_part(m, k, rows, EXTRA),
            g_raw.at[pl.ds(at * EXTRA, EXTRA)],
            g_sem.at[at],
        )

    order = [lead] + [m for m in range(lanes) if m != lead]
    for m in order:
        for k in range(planes):
            for copy in (g_copy(m, k), t_copy(m, k), s_copy(m, k)):
                copy.start()
    for m in order:
        for k in range(planes):
            at = m * planes + k
            g_copy(m, k).wait()
            line = g_raw[at * EXTRA : (at + 1) * EXTRA, :rows].astype(jnp.float32)[:1]
            g_row[:, at * rows : (at + 1) * rows] = jnp.broadcast_to(line, (8, rows))
            if m == lead:
                g_col[k * rows : (k + 1) * rows, :] = jnp.broadcast_to(line, (128, rows)).T
    total[...] = jnp.zeros_like(total)
    side = min(panel, 512)
    steps = panel // side
    group = side // rows

    for m in order:
        for k in range(planes):
            t_copy(m, k).wait()
            s_copy(m, k).wait()

        def one_row(it, m=m):
            at_i = pl.multiple_of(it * side, side)
            rows_t = t_all[pl.ds(lead * panel + at_i, side), :]
            col = g_col[pl.ds(at_i, side), :]

            def one_tile(jt):
                at_j = pl.multiple_of(m * panel + jt * side, side)
                teach = nt(rows_t, t_all[pl.ds(at_j, side), :]) * (-1.0 / width)
                students = s_all[pl.ds(at_j, side), :]
                line = g_row[:1, pl.ds(at_j, side)]
                same = jnp.concatenate([col] * (side // 128), 1) == line
                terms = []
                for k in range(group):
                    mine = here ^ (it * group + k)
                    weights = []
                    for other in range(group):
                        theirs = here ^ (jt * group + other)
                        both = mask[mine, theirs] + mask[theirs, mine]
                        weights.append(jnp.full((1, rows), both.astype(jnp.float32)))
                    weight = jnp.concatenate(weights, 1)
                    factor = jnp.where(same[k * rows : (k + 1) * rows], 2.0 * weight, weight)
                    error = teach[k * rows : (k + 1) * rows]
                    if own and k == 0:
                        stud = nt(s_all[:rows, :], students) * (1.0 / out)
                        if steps > 1:
                            stud = jnp.where(it == 0, stud, 0.0)
                        error = error + stud
                    terms.append((factor * error).astype(jnp.bfloat16))
                term = jnp.concatenate(terms, 0)
                total[pl.ds(at_i, side), :] += jnp.dot(
                    term, students, preferred_element_type=jnp.float32
                )

            loop(steps, one_tile)

        loop(steps, one_row)
    result[...] = total[...].astype(result.dtype)
    if own:
        keep = t_keep.shape[1]
        for c in range(2):

            @pl.when(place[1] % 2 == c)
            def _(c=c):
                t_keep[...] = t_all[:, c * keep : (c + 1) * keep]


def pair_values_kernel(planes, lanes, rows, out, width, own, chosen, mask, place, *refs):
    pieces = planes * lanes
    prow = rows + EXTRA
    t_in, s_in = refs[:pieces], refs[pieces : pieces + 2 * lanes]
    result = refs[pieces + 2 * lanes]
    here = place[0]
    lead = 0 if own else FAR

    def joined(parts, axis=0):
        return jnp.concatenate(list(parts), axis)

    def panel_of(m, some=range(planes)):
        return joined(t_in[m * planes + k][...] for k in some)

    def s_part(m, k, first, count):
        late = k >= NEAR
        at = (k - late * NEAR) * prow + first
        return s_in[2 * m + late][at : at + count, :]

    def students_of(m):
        return joined(s_part(m, k, 0, rows) for k in range(planes))

    def groups_of(m, k):
        return s_part(m, k, rows, EXTRA)[:, :rows].astype(jnp.float32)[:1]

    weights = []
    for k in chosen:
        scalars = [mask[here ^ k, here ^ j] + mask[here ^ j, here ^ k] for j in range(planes)]
        line = [jnp.full((1, rows), one.astype(jnp.float32) * (-1.0 / width)) for one in scalars]
        weights.append(joined(line, 1))
    column = joined(jnp.broadcast_to(groups_of(lead, k), (128, rows)).T for k in chosen)
    column = joined([column] * (planes * rows // 128), 1)
    lead_t = panel_of(lead, chosen)
    total = jnp.zeros((len(chosen) * rows, out), jnp.float32)
    for m in [lead] + [m for m in range(lanes) if m != lead]:
        students = students_of(m)
        teach = nt(lead_t, panel_of(m))
        same = column == joined((groups_of(m, k) for k in range(planes)), 1)
        terms = []
        for place_at, k in enumerate(chosen):
            span = slice(place_at * rows, (place_at + 1) * rows)
            weight = weights[place_at]
            error = teach[span]
            if own and k == 0:
                error = error - nt(s_in[0][:rows, :], students) * (width / out)
            factor = jnp.where(same[span], 2.0 * weight, weight)
            terms.append((factor * error).astype(jnp.bfloat16))
        total = total + jnp.dot(joined(terms), students, preferred_element_type=jnp.float32)
    result[...] = total.astype(result.dtype)
    if own:
        t_keep = refs[pieces + 2 * lanes + 1]
        keep = t_keep.shape[1]
        for c in range(2):

            @pl.when(place[1] % 2 == c)
            def _(c=c):
                for at in range(pieces):
                    t_keep[at * rows : (at + 1) * rows, :] = t_in[at][:, c * keep : (c + 1) * keep]


def hold_kernel(*refs):
    half = len(refs) // 2
    for source, target in zip(refs[:half], refs[half:]):
        target[...] = source[...]


def flip_kernel(value, result):
    result[...] = value[...].T


def last_kernel(planes, lanes, rows, t_keep, *refs):
    g_in, result = refs[:4], refs[4]
    total = None
    for at in range(4):
        count = NEAR if at < 2 else planes - NEAR
        for far in range(lanes // 2):
            first = (2 * far + at % 2) * planes + (at >= 2) * NEAR
            one = jnp.dot(
                t_keep[:, first * rows : (first + count) * rows],
                g_in[at][far * count * rows : (far + 1) * count * rows, :],
                preferred_element_type=jnp.float32,
            )
            total = one if total is None else total + one
    result[...] = total


def per_device(teacher, weight, block_mask, item_group):
    rows, width = teacher.shape
    out = weight.shape[1]
    planes = lax.axis_size("wide")
    lanes = lax.axis_size("narrow")
    plane = lax.axis_index("wide")
    lane = lax.axis_index("narrow")
    cols = width // planes
    part = cols // 2
    keep = cols // lanes
    items = rows * planes * lanes
    panel = rows * planes
    pieces = planes * lanes
    here = jnp.stack([plane, lane]).astype(jnp.int32)
    half = planes // 2

    def cut(k, side):
        start = (plane ^ k) * cols + (lane // 2 ^ side) * part
        return lax.dynamic_slice_in_dim(teacher, start, part, 1)

    mine = [cut(k, 0) for k in range(planes)]
    theirs = jnp.concatenate([cut(k, 1) for k in range(planes)], 0)
    got = swapped(theirs, "narrow", FAR)
    got = [got[k * rows : (k + 1) * rows] for k in range(planes)]
    own_core = swapped(mine[0], "narrow", CORE)
    first = [mine[0]] + [swapped(mine[k], "wide", k) for k in range(1, planes)]
    second = [got[0]] + [swapped(got[k], "wide", k) for k in range(1, planes)]

    low_weight = weight.astype(jnp.bfloat16)
    student = jnp.dot(
        after(teacher, own_core), low_weight, preferred_element_type=jnp.float32
    ).astype(jnp.bfloat16)
    extra = jnp.zeros((EXTRA, out), jnp.bfloat16).at[0, :rows].set(item_group.astype(jnp.bfloat16))
    packed = jnp.concatenate([student, extra], 0)

    s_of = {0: packed}
    bit = half
    while bit:
        for k in sorted(s_of):
            s_of[k ^ bit] = swapped(s_of[k], "wide", bit)
        bit //= 2
    s_all = [None] * lanes * 2
    for part_at, odd in enumerate((0, 1)):
        own = jnp.concatenate([s_of[k] for k in range(planes) if (k >= NEAR) == odd], 0)
        far = swapped(own, "narrow", FAR)
        for m, value in ((0, own), (FAR, far)):
            s_all[2 * m + part_at] = value
            s_all[2 * (m ^ CORE) + part_at] = swapped(value, "narrow", CORE)

    t_all = [*first, own_core, *(swapped(t, "narrow", CORE) for t in first[1:])]
    t_all += [*second, *(swapped(t, "narrow", CORE) for t in second)]

    late = 2 * planes
    t_all[late:] = pl.pallas_call(
        hold_kernel,
        out_shape=[jax.ShapeDtypeStruct((rows, part), jnp.bfloat16)] * late,
        in_specs=[VMEM] * late,
        out_specs=[VMEM] * late,
        compiler_params=pltpu.CompilerParams(vmem_limit_bytes=vmem_room(8 * late * rows * part)),
        cost_estimate=cost(0, HELD),
        name="hold",
    )(*t_all[late:])

    whole_tiles = pieces <= 16 and panel <= 512

    def pairs(own, chosen):
        chosen = tuple(chosen)
        some = len(chosen) * rows
        shapes = [jax.ShapeDtypeStruct((some, out), jnp.float32 if own else jnp.bfloat16)]
        if own:
            shapes.append(jax.ShapeDtypeStruct((items, keep), jnp.bfloat16))
        held = items * (2 * part + 2 * out) + 4 * panel * out
        if whole_tiles:
            return pl.pallas_call(
                functools.partial(pair_values_kernel, planes, lanes, rows, out, width, own, chosen),
                out_shape=shapes,
                in_specs=[SMEM, SMEM] + [VMEM] * (pieces + 2 * lanes),
                out_specs=[VMEM] * len(shapes),
                compiler_params=pltpu.CompilerParams(vmem_limit_bytes=vmem_room(held)),
                cost_estimate=cost(2 * some * items * (part + out), 2 * items * (part + out)),
                name="pairs_own" if own else "pairs_far",
            )(block_mask, here, *t_all, *s_all)
        return pl.pallas_call(
            functools.partial(pair_kernel, planes, lanes, rows, out, width, own),
            out_shape=shapes,
            in_specs=[SMEM, SMEM] + [ANY] * (pieces + 2 * lanes),
            out_specs=[VMEM] * len(shapes),
            scratch_shapes=[
                pltpu.VMEM((items, part), jnp.bfloat16),
                pltpu.VMEM((items, out), jnp.bfloat16),
                pltpu.VMEM((pieces * EXTRA, out), jnp.bfloat16),
                pltpu.VMEM((8, items), jnp.float32),
                pltpu.VMEM((panel, 128), jnp.float32),
                pltpu.VMEM((panel, out), jnp.float32),
                pltpu.SemaphoreType.DMA((pieces,)),
                pltpu.SemaphoreType.DMA((pieces,)),
                pltpu.SemaphoreType.DMA((pieces,)),
            ],
            compiler_params=pltpu.CompilerParams(vmem_limit_bytes=vmem_room(held)),
            cost_estimate=cost(2 * panel * items * (part + out), 2 * items * (part + out)),
            name="pairs_own" if own else "pairs_far",
        )(block_mask, here, *t_all, *s_all)

    if whole_tiles:
        (far_high,) = pairs(False, range(1, planes))
        far_high = swapped(far_high, "narrow", FAR)
        (far_low,) = pairs(False, range(1))
    else:
        (far_all,) = pairs(False, range(planes))
        far_high = swapped(far_all[rows:], "narrow", FAR)
        far_low = far_all[:rows]
    own_sum, t_keep = pairs(True, range(planes))
    far_low = swapped(after(far_low, own_sum), "narrow", FAR)
    sums_high = own_sum[rows:] + far_high.astype(jnp.float32)
    sums_low = own_sum[:rows] + far_low.astype(jnp.float32)
    t_keep = pl.pallas_call(
        flip_kernel,
        out_shape=jax.ShapeDtypeStruct((keep, items), jnp.bfloat16),
        in_specs=[VMEM],
        out_specs=VMEM,
        compiler_params=pltpu.CompilerParams(vmem_limit_bytes=vmem_room(4 * items * keep)),
        cost_estimate=cost(0, 4 * items * keep),
        name="flip",
    )(t_keep)

    grad = after(sums_low, t_keep)
    for k in range(1, planes):
        piece = sums_high[(k - 1) * rows : k * rows].astype(jnp.bfloat16)
        grad = grad + swapped(piece, "wide", k).astype(jnp.float32)
    coef = 2.0 * width / (items * out)
    grad = (grad * coef).astype(jnp.bfloat16)
    g_parts = [swapped(grad, "wide", k) for k in range(1, planes)]
    g_near = jnp.concatenate([grad, *g_parts[: NEAR - 1]], 0)
    g_near = jnp.concatenate([g_near, swapped(g_near, "narrow", FAR)], 0)
    g_rest = jnp.concatenate(g_parts[NEAR - 1 :], 0)
    g_rest = jnp.concatenate([g_rest, swapped(g_rest, "narrow", FAR)], 0)
    g_all = [g_near, swapped(g_near, "narrow", CORE), g_rest, swapped(g_rest, "narrow", CORE)]
    return pl.pallas_call(
        functools.partial(last_kernel, planes, lanes, rows),
        out_shape=jax.ShapeDtypeStruct((keep, out), jnp.float32),
        in_specs=[VMEM] * 5,
        out_specs=VMEM,
        compiler_params=pltpu.CompilerParams(vmem_limit_bytes=vmem_room(4 * items * (out + keep))),
        cost_estimate=cost(2 * items * keep * out, 2 * items * (keep + out)),
        name="last",
    )(t_keep, *g_all)


def solution(mesh):
    in_specs = (
        P(("parts", "wide", "narrow"), None),
        P(),
        P("parts", None),
        P(("parts", "wide", "narrow")),
    )
    out_specs = P(("parts", "wide", "narrow"), None)
    return jax.shard_map(
        per_device, mesh=mesh, in_specs=in_specs, out_specs=out_specs, check_vma=False
    )
```

```python
import functools

import jax
import jax.numpy as jnp
from jax import lax
from jax.experimental import pallas as pl
from jax.experimental.pallas import tpu as pltpu
from jax.sharding import PartitionSpec as P

ANY = pl.BlockSpec(memory_space=pl.ANY)
VMEM = pl.BlockSpec(memory_space=pltpu.VMEM)
SMEM = pl.BlockSpec(memory_space=pltpu.SMEM)
MIB = 1024 * 1024
EXTRA = 16
FAR, CORE = 2, 1
HELD = 72_000_000
NEAR = 2


def swapped(value, axis, bit):
    count = lax.axis_size(axis)
    return lax.ppermute(value, axis, [(source, source ^ bit) for source in range(count)])


def after(value, *others):
    return lax.optimization_barrier((value, *others))[0]


def vmem_room(held):
    return held + 14 * MIB


def cost(flops, moved):
    return pl.CostEstimate(flops=flops, bytes_accessed=moved, transcendentals=0)


def nt(a, b):
    return lax.dot_general(a, b, (((1,), (1,)), ((), ())), preferred_element_type=jnp.float32)


def loop(count, body):
    if count <= 4:
        for step in range(count):
            body(step)
    else:
        lax.fori_loop(0, count, lambda step, carry: (body(step), carry)[1], 0)


def pair_kernel(planes, lanes, rows, out, width, own, mask, place, *refs):
    pieces = planes * lanes
    panel = planes * rows
    prow = rows + EXTRA
    t_in, s_in = refs[:pieces], refs[pieces : pieces + 2 * lanes]
    result = refs[pieces + 2 * lanes]
    rest = list(refs[pieces + 2 * lanes + 1 :])
    t_keep = rest.pop(0) if own else None
    t_all, s_all, g_raw, g_row, g_col, total, t_sem, s_sem, g_sem = rest
    here = place[0]
    lead = 0 if own else FAR

    def t_copy(m, k):
        at = m * planes + k
        return pltpu.make_async_copy(t_in[at], t_all.at[pl.ds(at * rows, rows)], t_sem.at[at])

    def s_part(m, k, first, count):
        late = k >= NEAR
        return s_in[2 * m + late].at[pl.ds((k - late * NEAR) * prow + first, count)]

    def s_copy(m, k):
        at = m * planes + k
        return pltpu.make_async_copy(
            s_part(m, k, 0, rows), s_all.at[pl.ds(at * rows, rows)], s_sem.at[at]
        )

    def g_copy(m, k):
        at = m * planes + k
        return pltpu.make_async_copy(
            s_part(m, k, rows, EXTRA),
            g_raw.at[pl.ds(at * EXTRA, EXTRA)],
            g_sem.at[at],
        )

    order = [lead] + [m for m in range(lanes) if m != lead]
    for m in order:
        for k in range(planes):
            for copy in (g_copy(m, k), t_copy(m, k), s_copy(m, k)):
                copy.start()
    for m in order:
        for k in range(planes):
            at = m * planes + k
            g_copy(m, k).wait()
            line = g_raw[at * EXTRA : (at + 1) * EXTRA, :rows].astype(jnp.float32)[:1]
            g_row[:, at * rows : (at + 1) * rows] = jnp.broadcast_to(line, (8, rows))
            if m == lead:
                g_col[k * rows : (k + 1) * rows, :] = jnp.broadcast_to(line, (128, rows)).T
    total[...] = jnp.zeros_like(total)
    side = min(panel, 512)
    steps = panel // side
    group = side // rows

    for m in order:
        for k in range(planes):
            t_copy(m, k).wait()
            s_copy(m, k).wait()

        def one_row(it, m=m):
            at_i = pl.multiple_of(it * side, side)
            rows_t = t_all[pl.ds(lead * panel + at_i, side), :]
            col = g_col[pl.ds(at_i, side), :]

            def one_tile(jt):
                at_j = pl.multiple_of(m * panel + jt * side, side)
                teach = nt(rows_t, t_all[pl.ds(at_j, side), :]) * (-1.0 / width)
                students = s_all[pl.ds(at_j, side), :]
                line = g_row[:1, pl.ds(at_j, side)]
                same = jnp.concatenate([col] * (side // 128), 1) == line
                terms = []
                for k in range(group):
                    mine = here ^ (it * group + k)
                    weights = []
                    for other in range(group):
                        theirs = here ^ (jt * group + other)
                        both = mask[mine, theirs] + mask[theirs, mine]
                        weights.append(jnp.full((1, rows), both.astype(jnp.float32)))
                    weight = jnp.concatenate(weights, 1)
                    factor = jnp.where(same[k * rows : (k + 1) * rows], 2.0 * weight, weight)
                    error = teach[k * rows : (k + 1) * rows]
                    if own and k == 0:
                        stud = nt(s_all[:rows, :], students) * (1.0 / out)
                        if steps > 1:
                            stud = jnp.where(it == 0, stud, 0.0)
                        error = error + stud
                    terms.append((factor * error).astype(jnp.bfloat16))
                term = jnp.concatenate(terms, 0)
                total[pl.ds(at_i, side), :] += jnp.dot(
                    term, students, preferred_element_type=jnp.float32
                )

            loop(steps, one_tile)

        loop(steps, one_row)
    result[...] = total[...].astype(result.dtype)
    if own:
        keep = t_keep.shape[1]
        for c in range(2):

            @pl.when(place[1] % 2 == c)
            def _(c=c):
                t_keep[...] = t_all[:, c * keep : (c + 1) * keep]


def pair_values_kernel(planes, lanes, rows, out, width, own, chosen, mask, place, *refs):
    pieces = planes * lanes
    prow = rows + EXTRA
    t_in, s_in = refs[:pieces], refs[pieces : pieces + 2 * lanes]
    result = refs[pieces + 2 * lanes]
    here = place[0]
    lead = 0 if own else FAR

    def joined(parts, axis=0):
        return jnp.concatenate(list(parts), axis)

    def panel_of(m, some=range(planes)):
        return joined(t_in[m * planes + k][...] for k in some)

    def s_part(m, k, first, count):
        late = k >= NEAR
        at = (k - late * NEAR) * prow + first
        return s_in[2 * m + late][at : at + count, :]

    def students_of(m):
        return joined(s_part(m, k, 0, rows) for k in range(planes))

    def groups_of(m, k):
        return s_part(m, k, rows, EXTRA)[:, :rows].astype(jnp.float32)[:1]

    weights = []
    for k in chosen:
        scalars = [mask[here ^ k, here ^ j] + mask[here ^ j, here ^ k] for j in range(planes)]
        line = [jnp.full((1, rows), one.astype(jnp.float32) * (-1.0 / width)) for one in scalars]
        weights.append(joined(line, 1))
    column = joined(jnp.broadcast_to(groups_of(lead, k), (128, rows)).T for k in chosen)
    column = joined([column] * (planes * rows // 128), 1)
    lead_t = panel_of(lead, chosen)
    total = jnp.zeros((len(chosen) * rows, out), jnp.float32)
    for m in [lead] + [m for m in range(lanes) if m != lead]:
        students = students_of(m)
        teach = nt(lead_t, panel_of(m))
        same = column == joined((groups_of(m, k) for k in range(planes)), 1)
        terms = []
        for place_at, k in enumerate(chosen):
            span = slice(place_at * rows, (place_at + 1) * rows)
            weight = weights[place_at]
            error = teach[span]
            if own and k == 0:
                error = error - nt(s_in[0][:rows, :], students) * (width / out)
            factor = jnp.where(same[span], 2.0 * weight, weight)
            terms.append((factor * error).astype(jnp.bfloat16))
        total = total + jnp.dot(joined(terms), students, preferred_element_type=jnp.float32)
    result[...] = total.astype(result.dtype)
    if own:
        t_keep = refs[pieces + 2 * lanes + 1]
        keep = t_keep.shape[1]
        for c in range(2):

            @pl.when(place[1] % 2 == c)
            def _(c=c):
                for at in range(pieces):
                    t_keep[at * rows : (at + 1) * rows, :] = t_in[at][:, c * keep : (c + 1) * keep]


def hold_kernel(*refs):
    half = len(refs) // 2
    for source, target in zip(refs[:half], refs[half:]):
        target[...] = source[...]


def flip_kernel(value, result):
    result[...] = value[...].T


def last_kernel(planes, lanes, rows, start, count, t_keep, *refs):
    g_in, result = refs[:2], refs[-1]
    total = refs[2][...] if len(refs) == 4 else None
    for at in range(2):
        for far in range(lanes // 2):
            first = (2 * far + at) * planes + start
            one = jnp.dot(
                t_keep[:, first * rows : (first + count) * rows],
                g_in[at][far * count * rows : (far + 1) * count * rows, :],
                preferred_element_type=jnp.float32,
            )
            total = one if total is None else total + one
    result[...] = total


def per_device(teacher, weight, block_mask, item_group):
    rows, width = teacher.shape
    out = weight.shape[1]
    planes = lax.axis_size("wide")
    lanes = lax.axis_size("narrow")
    plane = lax.axis_index("wide")
    lane = lax.axis_index("narrow")
    cols = width // planes
    part = cols // 2
    keep = cols // lanes
    items = rows * planes * lanes
    panel = rows * planes
    pieces = planes * lanes
    here = jnp.stack([plane, lane]).astype(jnp.int32)
    half = planes // 2

    def cut(k, side):
        start = (plane ^ k) * cols + (lane // 2 ^ side) * part
        return lax.dynamic_slice_in_dim(teacher, start, part, 1)

    mine = [cut(k, 0) for k in range(planes)]
    theirs = jnp.concatenate([cut(k, 1) for k in range(planes)], 0)
    got = swapped(theirs, "narrow", FAR)
    got = [got[k * rows : (k + 1) * rows] for k in range(planes)]
    own_core = swapped(mine[0], "narrow", CORE)
    first = [mine[0]] + [swapped(mine[k], "wide", k) for k in range(1, planes)]
    second = [got[0]] + [swapped(got[k], "wide", k) for k in range(1, planes)]

    low_weight = weight.astype(jnp.bfloat16)
    student = jnp.dot(
        after(teacher, own_core), low_weight, preferred_element_type=jnp.float32
    ).astype(jnp.bfloat16)
    extra = jnp.zeros((EXTRA, out), jnp.bfloat16).at[0, :rows].set(item_group.astype(jnp.bfloat16))
    packed = jnp.concatenate([student, extra], 0)

    s_of = {0: packed}
    bit = half
    while bit:
        for k in sorted(s_of):
            s_of[k ^ bit] = swapped(s_of[k], "wide", bit)
        bit //= 2
    s_all = [None] * lanes * 2
    for part_at, odd in enumerate((0, 1)):
        own = jnp.concatenate([s_of[k] for k in range(planes) if (k >= NEAR) == odd], 0)
        far = swapped(own, "narrow", FAR)
        for m, value in ((0, own), (FAR, far)):
            s_all[2 * m + part_at] = value
            s_all[2 * (m ^ CORE) + part_at] = swapped(value, "narrow", CORE)

    t_all = [*first, own_core, *(swapped(t, "narrow", CORE) for t in first[1:])]
    t_all += [*second, *(swapped(t, "narrow", CORE) for t in second)]

    late = 2 * planes
    t_all[late:] = pl.pallas_call(
        hold_kernel,
        out_shape=[jax.ShapeDtypeStruct((rows, part), jnp.bfloat16)] * late,
        in_specs=[VMEM] * late,
        out_specs=[VMEM] * late,
        compiler_params=pltpu.CompilerParams(vmem_limit_bytes=vmem_room(8 * late * rows * part)),
        cost_estimate=cost(0, HELD),
        name="hold",
    )(*t_all[late:])

    whole_tiles = pieces <= 16 and panel <= 512

    def pairs(own, chosen):
        chosen = tuple(chosen)
        some = len(chosen) * rows
        shapes = [jax.ShapeDtypeStruct((some, out), jnp.float32 if own else jnp.bfloat16)]
        if own:
            shapes.append(jax.ShapeDtypeStruct((items, keep), jnp.bfloat16))
        held = items * (2 * part + 2 * out) + 4 * panel * out
        if whole_tiles:
            return pl.pallas_call(
                functools.partial(pair_values_kernel, planes, lanes, rows, out, width, own, chosen),
                out_shape=shapes,
                in_specs=[SMEM, SMEM] + [VMEM] * (pieces + 2 * lanes),
                out_specs=[VMEM] * len(shapes),
                compiler_params=pltpu.CompilerParams(vmem_limit_bytes=vmem_room(held)),
                cost_estimate=cost(2 * some * items * (part + out), 2 * items * (part + out)),
                name="pairs_own" if own else "pairs_far",
            )(block_mask, here, *t_all, *s_all)
        return pl.pallas_call(
            functools.partial(pair_kernel, planes, lanes, rows, out, width, own),
            out_shape=shapes,
            in_specs=[SMEM, SMEM] + [ANY] * (pieces + 2 * lanes),
            out_specs=[VMEM] * len(shapes),
            scratch_shapes=[
                pltpu.VMEM((items, part), jnp.bfloat16),
                pltpu.VMEM((items, out), jnp.bfloat16),
                pltpu.VMEM((pieces * EXTRA, out), jnp.bfloat16),
                pltpu.VMEM((8, items), jnp.float32),
                pltpu.VMEM((panel, 128), jnp.float32),
                pltpu.VMEM((panel, out), jnp.float32),
                pltpu.SemaphoreType.DMA((pieces,)),
                pltpu.SemaphoreType.DMA((pieces,)),
                pltpu.SemaphoreType.DMA((pieces,)),
            ],
            compiler_params=pltpu.CompilerParams(vmem_limit_bytes=vmem_room(held)),
            cost_estimate=cost(2 * panel * items * (part + out), 2 * items * (part + out)),
            name="pairs_own" if own else "pairs_far",
        )(block_mask, here, *t_all, *s_all)

    if whole_tiles:
        (far_high,) = pairs(False, range(1, planes))
        far_high = swapped(far_high, "narrow", FAR)
        (far_low,) = pairs(False, range(1))
    else:
        (far_all,) = pairs(False, range(planes))
        far_high = swapped(far_all[rows:], "narrow", FAR)
        far_low = far_all[:rows]
    own_sum, t_keep = pairs(True, range(planes))
    far_low = swapped(after(far_low, own_sum), "narrow", FAR)
    sums_high = own_sum[rows:] + far_high.astype(jnp.float32)
    sums_low = own_sum[:rows] + far_low.astype(jnp.float32)
    t_keep = pl.pallas_call(
        flip_kernel,
        out_shape=jax.ShapeDtypeStruct((keep, items), jnp.bfloat16),
        in_specs=[VMEM],
        out_specs=VMEM,
        compiler_params=pltpu.CompilerParams(vmem_limit_bytes=vmem_room(4 * items * keep)),
        cost_estimate=cost(0, 4 * items * keep),
        name="flip",
    )(t_keep)

    grad = after(sums_low, t_keep)
    for k in range(1, planes):
        piece = sums_high[(k - 1) * rows : k * rows].astype(jnp.bfloat16)
        grad = grad + swapped(piece, "wide", k).astype(jnp.float32)
    coef = 2.0 * width / (items * out)
    grad = (grad * coef).astype(jnp.bfloat16)
    g_parts = [swapped(grad, "wide", k) for k in range(1, planes)]
    g_near = jnp.concatenate([grad, *g_parts[: NEAR - 1]], 0)
    g_near = jnp.concatenate([g_near, swapped(g_near, "narrow", FAR)], 0)
    g_rest = jnp.concatenate(g_parts[NEAR - 1 :], 0)
    g_rest = jnp.concatenate([g_rest, swapped(g_rest, "narrow", FAR)], 0)
    g_all = [g_near, swapped(g_near, "narrow", CORE), g_rest, swapped(g_rest, "narrow", CORE)]
    def product(name, start, count, *operands):
        return pl.pallas_call(
            functools.partial(last_kernel, planes, lanes, rows, start, count),
            out_shape=jax.ShapeDtypeStruct((keep, out), jnp.float32),
            in_specs=[VMEM] * (1 + len(operands)),
            out_specs=VMEM,
            compiler_params=pltpu.CompilerParams(
                vmem_limit_bytes=vmem_room(4 * items * (out + keep))
            ),
            cost_estimate=cost(2 * lanes * count * rows * keep * out, 2 * items * (keep + out)),
            name=name,
        )(t_keep, *operands)

    rest = product("rest", NEAR, planes - NEAR, *g_all[2:])
    return product("last", 0, NEAR, *g_all[:2], rest)


def solution(mesh):
    in_specs = (
        P(("parts", "wide", "narrow"), None),
        P(),
        P("parts", None),
        P(("parts", "wide", "narrow")),
    )
    out_specs = P(("parts", "wide", "narrow"), None)
    return jax.shard_map(
        per_device, mesh=mesh, in_specs=in_specs, out_specs=out_specs, check_vma=False
    )
```
